32 devices in a mesh: section: 4 (over z), batch: 8 (over y, x, core).
Axes of the slice: x: 2, y: 2, z: 4, core: 2. Of those that a mesh axis runs over, the one named last changes fastest.
Arguments:
- images: bfloat16 [8, 256, 1536], P('batch'), may hold values from -10 to 10
- weights: bfloat16 [4, 6, 256, 256], P('section'), may hold values from -0.375 to 0.375
- bn_mean: float32 [4, 1536], P('section'), may hold values from -3 to 3
- bn_var: float32 [4, 1536], P('section'), may hold values from 0.25 to 2
- bn_gain: float32 [4, 1536], P('section'), may hold values from 0.1 to 1.9
- bn_bias: float32 [4, 1536], P('section'), may hold values from -3 to 3
Outputs:
- image_grad: bfloat16 [8, 256, 1536], P('batch', 'section')
- loss_value: float32 [], replicated
The draws below stay inside these ranges and needn't reach their ends.
All inputs are finite; a program needn't handle non-finite values.
Results may differ from the reference program's by a relative error of at most 0.013.
Values may be sent and summed in bfloat16 or wider, within the bound.
A program may use at most 64 MiB of HBM per device.

```python
import math
import jax
import jax.numpy as jnp
from jax import lax

CW = 1536
GW = 256
BLOCK = 512
MICRO = 8
ROWS = 32
LAYERS = 4
N_BATCH = 8


def draw_images(key, part):
    key_noise = jax.random.fold_in(key, 11)
    key_offset = jax.random.fold_in(key, 23)
    key_mixing = jax.random.fold_in(key, 53)
    shape = (N_BATCH, MICRO * ROWS, CW)
    block_count = CW // BLOCK
    offsets = jnp.clip(jax.random.normal(key_offset, (CW,), jnp.float32), -3.0, 3.0)
    ramp = jnp.arange(N_BATCH, dtype=jnp.float32) / max(N_BATCH - 1, 1)
    mix_noise = jnp.clip(jax.random.normal(key_mixing, (block_count, BLOCK, BLOCK), jnp.float32), -4.0, 4.0)
    mixing = jnp.eye(BLOCK, dtype=jnp.float32)[None] + mix_noise * (0.6 / BLOCK ** 0.5)
    noise = jnp.clip(jax.random.normal(key_noise, shape, jnp.float32), -6.0, 6.0) * 0.8
    factor = 0.3 + 1.2 * ramp
    blocks = noise.reshape(N_BATCH, MICRO * ROWS, block_count, BLOCK)
    mixed = jnp.einsum('nrbi,bij->nrbj', blocks, mixing, precision=lax.Precision.HIGHEST).reshape(shape)
    values = jnp.clip(mixed + factor[:, None, None] * offsets[None, None, :], -9.9, 9.9)
    return values.astype(jnp.bfloat16)


def block_levels(rng, shape, cuts, smallest, high):
    def one(axis_at, shards_of):
        draws = jax.random.uniform(jax.random.fold_in(jax.random.fold_in(rng, 6), axis_at), (shards_of,), jnp.float32, smallest / len(cuts), high / len(cuts))
        return jnp.repeat(jnp.exp(draws), shape[axis_at] // shards_of).reshape((-1,) + (1,) * (len(shape) - axis_at - 1))

    factor_of = one(*cuts[0])
    for cut in cuts[1:]:
        factor_of = factor_of * one(*cut)
    return factor_of


def centred(stream_key, dims, width, limit, cuts=(), kind=jnp.bfloat16):
    array = width * jax.random.normal(stream_key, dims, jnp.float32)
    if cuts:
        array = array * block_levels(stream_key, dims, cuts, -0.22, 0.18)
    return jnp.clip(array, -limit, limit).astype(kind)


def setup_inputs(seed: int = 0) -> dict:
    arg_keys = jax.random.split(jax.random.key(seed), 7)
    images = draw_images(jax.random.fold_in(arg_keys[6], 71), 0)
    weights = centred(arg_keys[1], (LAYERS, CW // GW, GW, GW), GW ** -0.5, 0.375, ((0, 4),))
    bn_mean = centred(arg_keys[2], (LAYERS, CW), 0.5, 3.0, ((0, 4),), jnp.float32)
    bn_var = jnp.clip(jnp.exp(math.log(2.0) - 2.0794415 * jax.random.uniform(arg_keys[3], (LAYERS, CW), jnp.float32) ** block_levels(arg_keys[3], (LAYERS, CW), ((0, 4),), -0.2, 0.2)), 0.25, 2.0)
    bn_gain = jnp.clip(1.0 + 0.18 * jax.random.normal(arg_keys[4], (LAYERS, CW), jnp.float32), 0.1, 1.9)
    bn_bias = centred(arg_keys[5], (LAYERS, CW), 0.5, 3.0, ((0, 4),), jnp.float32)
    return dict(images=images, weights=weights, bn_mean=bn_mean, bn_var=bn_var, bn_gain=bn_gain, bn_bias=bn_bias)


EPS = 1e-05
HIGHEST = lax.Precision.HIGHEST

def conv_forward(hidden, weight):
    row_total = hidden.shape[0]
    groups, in_width, out_width = weight.shape
    pieces = hidden.astype(jnp.float32).reshape(row_total, groups, in_width)
    result = jnp.einsum('rgi,gio->rgo', pieces, weight.astype(jnp.float32))
    return result.reshape(row_total, groups * out_width)

def conv_backward(upstream, weight):
    row_total = upstream.shape[0]
    groups, in_width, out_width = weight.shape
    pieces = upstream.astype(jnp.float32).reshape(row_total, groups, out_width)
    result = jnp.einsum('rgo,gio->rgi', pieces, weight.astype(jnp.float32))
    return result.reshape(row_total, groups * in_width)

def target_blocks(variance):
    blocks = variance.reshape(-1, BLOCK)
    return blocks[:, :, None] * jnp.eye(BLOCK, dtype=jnp.float32)[None]

def reference(images, weights, bn_mean, bn_var, bn_gain, bn_bias):
    channels = images.shape[2]
    hidden = images.reshape(-1, channels)
    row_total = hidden.shape[0]
    block_count = channels // BLOCK
    saved = []
    loss_total = jnp.zeros((), jnp.float32)
    for layer_index in range(LAYERS):
        bn_scale = bn_gain[layer_index] * lax.rsqrt(bn_var[layer_index] + EPS)
        pre_act = conv_forward(hidden, weights[layer_index])
        batch_mean = lax.optimization_barrier(jnp.sum(pre_act, axis=0)) / row_total
        centered = (pre_act - batch_mean).reshape(row_total, block_count, BLOCK)
        covariance = jnp.einsum('rbi,rbj->bij', centered, centered, precision=HIGHEST) / row_total
        deviation = covariance - target_blocks(bn_var[layer_index])
        loss_total = loss_total + jnp.sum((batch_mean - bn_mean[layer_index]) ** 2) + 0.25 * jnp.sum(deviation ** 2)
        saved.append((pre_act, batch_mean, deviation, bn_scale))
        active = (pre_act - bn_mean[layer_index]) * bn_scale + bn_bias[layer_index]
        hidden = jax.nn.silu(active).astype(jnp.bfloat16)
    upstream = jnp.zeros((row_total, channels), jnp.bfloat16)
    for layer_index in reversed(range(LAYERS)):
        pre_act, batch_mean, deviation, bn_scale = saved[layer_index]
        active = (pre_act - bn_mean[layer_index]) * bn_scale + bn_bias[layer_index]
        sig_value = jax.nn.sigmoid(active)
        silu_slope = sig_value * (1.0 + active * (1.0 - sig_value))
        centered = (pre_act - batch_mean).reshape(row_total, block_count, BLOCK)
        cov_pull = jnp.einsum('rbi,bij->rbj', centered, deviation, precision=HIGHEST).reshape(row_total, channels)
        pre_grad = upstream.astype(jnp.float32) * silu_slope * bn_scale + 2.0 * (batch_mean - bn_mean[layer_index]) + cov_pull
        pre_grad = pre_grad.astype(jnp.bfloat16)
        upstream = conv_backward(pre_grad, weights[layer_index]).astype(jnp.bfloat16)
    return (upstream.reshape(images.shape), loss_total / (LAYERS * channels))
```

```python
import functools

import jax
import jax.numpy as jnp
from jax import lax
from jax.experimental import pallas as pl
from jax.experimental.pallas import tpu as pltpu
from jax.sharding import PartitionSpec as P

BLOCK = 512
GROUP = 256
HALF = 128
WIDE = GROUP + HALF
LAG = (0, 0, 0, 1, 2, 3, 4, 4)
EPS = 1e-05
MESH = pl.DeviceIdType.MESH
F32 = jnp.float32
BF16 = jnp.bfloat16


def dot(a, b, dims):
    return lax.dot_general(a, b, (dims, ((), ())), preferred_element_type=F32)


def kernel(nl, nb, nj, x_ref, w_ref, mean_ref, var_ref, gain_ref, bias_ref, out_ref, loss_ref,
           wall, ss, xbuf, zall, slope, zc, sacc, srs, rs, e, psend, pall, mub, mu_all, lossb, lossz,
           z_s, z_r, ss_s, ss_r, w2_s, w2_r, w3_s, w3_r, zc_s, zc_r, mu_s, mu_r, rs_s, rs_r,
           ag_s, ag_r, ex_s, ex_r, pu_s, pu_r, lb_s, lb_r, lz_s, lz_r):
    s = lax.axis_index("section")
    b = lax.axis_index("batch")
    chip, core = b // 2, b % 2
    nc = nb // 2
    mate = chip * 2 + (1 - core)
    rows = x_ref.shape[0]
    own_rows = rows // nl
    piece = GROUP // nc
    row_total = rows * nb

    def copy(src, dst, ssem, rsem, sec, bat):
        return pltpu.make_async_remote_copy(
            src_ref=src, dst_ref=dst, send_sem=ssem, recv_sem=rsem,
            device_id=(sec, bat), device_id_type=MESH)

    def each(count, me, body):
        def step(k, carry):
            body(k, lax.rem(me + k, count))
            return carry
        lax.fori_loop(1, count, step, 0)

    def z_copy(j, k, q):
        return copy(w_ref.at[j, chip, core], wall.at[s, j, chip, core], z_s.at[j, k], z_r.at[j, s], q, b)

    def z_wait(j, l):
        d = wall.at[l, j, chip, core]
        copy(d, d, z_s.at[j, 0], z_r.at[j, l], l, b).wait_recv()

    def ss_copy(k, q):
        return copy(ss.at[s], ss.at[s], ss_s.at[k], ss_r.at[s], q, b)

    def w2_copy(l, j, k, q):
        d = wall.at[l, j, chip, core]
        return copy(d, d, w2_s.at[l, j, k], w2_r.at[l, j, chip], s, q * 2 + core)

    def w3_copy(l, j, half):
        d = wall.at[l, j, :, half]
        return copy(d, d, w3_s.at[l, j], w3_r.at[l, j], s, mate)

    def zc_copy(j, half):
        return copy(zc.at[j, half], zc.at[j, half], zc_s.at[j], zc_r.at[j], s, mate)

    def mu_copy(j, k, q):
        return copy(mub.at[j, b], mub.at[j, b], mu_s.at[j, k], mu_r.at[j, b], s, q)

    def rs_copy(j, k, q):
        return copy(srs.at[j, q], rs.at[j, chip], rs_s.at[j, k], rs_r.at[j, chip], s, q * 2 + core)

    def ag_copy(j, k, q):
        d = e.at[j, core, chip]
        return copy(d, d, ag_s.at[j, k], ag_r.at[j, chip], s, q * 2 + core)

    def ex_copy(j, half):
        return copy(e.at[j, half], e.at[j, half], ex_s.at[j], ex_r.at[j], s, mate)

    def pu_copy(j, k, q):
        return copy(psend.at[j, q], pall.at[s, j], pu_s.at[j, k], pu_r.at[j, s], q, b)

    def lb_copy(k, q):
        return copy(lossb.at[b], lossb.at[b], lb_s.at[k], lb_r.at[b], s, q)

    def lz_copy(k, q):
        return copy(lossz.at[s], lossz.at[s], lz_s.at[k], lz_r.at[s], q, b)

    barrier = pltpu.get_barrier_semaphore()
    each(nb, b, lambda k, q: pl.semaphore_signal(barrier, inc=1, device_id=(s, q), device_id_type=MESH))
    each(nl, s, lambda k, q: pl.semaphore_signal(barrier, inc=1, device_id=(q, b), device_id_type=MESH))
    scale_own = gain_ref[...] * lax.rsqrt(var_ref[...] + EPS)
    ss[s, 0:1, :] = 0.5 * scale_own
    ss[s, 1:2, :] = 0.5 * (bias_ref[...] - mean_ref[...] * scale_own)
    for j in range(nj):
        wall[s, j] = w_ref[j]
    pl.semaphore_wait(barrier, nb - 1 + nl - 1)

    each(nl, s, lambda k, q: ss_copy(k, q).start())
    for j in range(nj):
        each(nl, s, lambda k, q: z_copy(j, k, q).start())

    def spread_chips(j):
        def one(_, l):
            z_wait(j, l)
            each(nc, chip, lambda k, q: w2_copy(l, j, k, q).start())
        each(nl, s, one)

    def spread_mate(j):
        def one(_, l):
            def arrived(k, q):
                d = wall.at[l, j, q, core]
                copy(d, d, w2_s.at[l, j, 0], w2_r.at[l, j, q], s, q * 2 + core).wait_recv()
            each(nc, chip, arrived)
            w3_copy(l, j, core).start()
        each(nl, s, one)

    def forward(j):
        cols = slice(j * BLOCK, (j + 1) * BLOCK)
        xbuf[...] = x_ref[:, cols]

        def layer(l, carry):
            @pl.when(l != s)
            def _():
                w3_copy(l, j, 1 - core).wait_recv()
                if j == 0:
                    copy(ss.at[l], ss.at[l], ss_s.at[0], ss_r.at[l], l, b).wait_recv()
            w = wall[l, j].reshape(BLOCK, GROUP)
            for g in range(BLOCK // GROUP):
                part = slice(g * GROUP, (g + 1) * GROUP)
                lanes = slice(j * BLOCK + g * GROUP, j * BLOCK + (g + 1) * GROUP)
                z = dot(xbuf[:, part], w[part], ((1,), (0,)))
                zall[l, j, :, part] = z
                half = z * ss[l, 0:1, lanes] + ss[l, 1:2, lanes]
                xbuf[:, part] = (half + half * jnp.tanh(half)).astype(BF16)
            return carry
        lax.fori_loop(0, nl, layer, 0)
        z = zall[s, j]
        mu = jnp.sum(z, axis=0, keepdims=True) * (1.0 / rows)
        mub[j, b] = mu
        each(nb, b, lambda k, q: mu_copy(j, k, q).start())
        centered = (z - mu).astype(BF16)
        for h in range(BLOCK // GROUP):
            zc[j, core, h] = centered[:, h * GROUP:(h + 1) * GROUP]
        zc_copy(j, core).start()

    def gram(j):
        zc_copy(j, 1 - core).wait_recv()
        cross = pl.ds(pl.multiple_of(core * HALF, HALF), HALF)
        square = dot(zc[j, 0, core], zc[j, 0, core], ((0,), (0,))) + dot(
            zc[j, 1, core], zc[j, 1, core], ((0,), (0,)))
        other = dot(zc[j, 0, 0], zc[j, 0, 1, :, cross], ((0,), (0,))) + dot(
            zc[j, 1, 0], zc[j, 1, 1, :, cross], ((0,), (0,)))
        total = jnp.concatenate([square, other], axis=1).reshape(nc, piece, WIDE)
        sacc[j] = total
        srs[j] = total.astype(BF16)
        each(nc, chip, lambda k, q: rs_copy(j, k, q).start())

    def batch_mean(j):
        return jnp.sum(mub[j], axis=0) * (1.0 / nb)

    def reduce(j):
        cols = slice(j * BLOCK, (j + 1) * BLOCK)

        def arrived_mu(k, q):
            copy(mub.at[j, q], mub.at[j, q], mu_s.at[j, 0], mu_r.at[j, q], s, q).wait_recv()
        each(nb, b, arrived_mu)
        mu = batch_mean(j)
        mine = pl.ds(pl.multiple_of(core * GROUP, GROUP), GROUP)
        cross = pl.ds(pl.multiple_of(GROUP + core * HALF, HALF), HALF)
        var_lanes = pl.ds(pl.multiple_of(j * BLOCK + core * GROUP, GROUP), GROUP)
        mu_all[...] = mu
        mu_mine, mu_cross, mu_low = mu_all[:, mine], mu_all[:, cross], mu[:, :GROUP]
        eye = (lax.broadcasted_iota(jnp.int32, (piece, GROUP), 0) + chip * piece
               == lax.broadcasted_iota(jnp.int32, (piece, GROUP), 1)).astype(F32)

        def between(i, acc):
            low = mub[j, i, :, :GROUP] - mu_low
            d_mine = mub[j, i, :, mine] - mu_mine
            d_cross = mub[j, i, :, cross] - mu_cross
            column = jnp.sum(eye * d_mine, axis=1, keepdims=True)
            column_low = jnp.sum(eye * low, axis=1, keepdims=True)
            return (acc[0] + column * d_mine, acc[1] + column_low * d_cross)
        corr = jnp.concatenate(lax.fori_loop(
            0, nb, between, (jnp.zeros((piece, GROUP), F32), jnp.zeros((piece, HALF), F32))), axis=1)
        sacc[j, chip] = sacc[j, chip] + corr * rows

        def arrived(k, q):
            copy(rs.at[j, q], rs.at[j, q], rs_s.at[j, 0], rs_r.at[j, q], s, q * 2 + core).wait_recv()
            sacc[j, chip] = sacc[j, chip] + rs[j, q].astype(F32)
        each(nc, chip, arrived)
        cov = sacc[j, chip] * (1.0 / row_total)
        dev, dev_cross = cov[:, :GROUP] - eye * var_ref[:, var_lanes], cov[:, GROUP:]
        e[j, core, chip] = jnp.concatenate([dev, dev_cross], axis=1).astype(BF16)
        each(nc, chip, lambda k, q: ag_copy(j, k, q).start())
        square = jnp.sum((dev * dev).reshape(piece // 8, 8, GROUP), axis=0) * 0.25
        double = jnp.sum((dev_cross * dev_cross).reshape(piece // 8, 8, HALF), axis=0) * 0.5
        off = mu - mean_ref[:, cols]
        off = off * off
        off = sum(off[:, i * HALF:(i + 1) * HALF] for i in range(BLOCK // HALF))
        head = (lax.broadcasted_iota(jnp.int32, (8, HALF), 0) + b == 0).astype(F32)
        tile = square[:, :HALF] + square[:, HALF:] + double + head * off
        if j == 0:
            lossb[b] = tile
        else:
            lossb[b] = lossb[b] + tile
        if j == nj - 1:
            each(nb, b, lambda k, q: lb_copy(k, q).start())

    def swap(j):
        def arrived(k, q):
            d = e.at[j, core, q]
            copy(d, d, ag_s.at[j, 0], ag_r.at[j, q], s, q * 2 + core).wait_recv()
        each(nc, chip, arrived)
        ex_copy(j, core).start()

    def pull(j):
        cols = slice(j * BLOCK, (j + 1) * BLOCK)
        mu = batch_mean(j)
        ex_copy(j, 1 - core).wait_recv()
        c0 = (zall[s, j, :, :GROUP] - mu[:, :GROUP]).astype(BF16)
        c1 = (zall[s, j, :, GROUP:] - mu[:, GROUP:]).astype(BF16)
        e0, e1 = e[j, 0].reshape(GROUP, WIDE), e[j, 1].reshape(GROUP, WIDE)
        cross = jnp.concatenate([e0[:, GROUP:], e1[:, GROUP:]], axis=1)
        p0 = dot(c0, e0[:, :GROUP], ((1,), (0,))) + dot(c1, cross, ((1,), (1,)))
        p1 = dot(c0, cross, ((1,), (0,))) + dot(c1, e1[:, :GROUP], ((1,), (0,)))
        p = jnp.concatenate([p0, p1], axis=1) + 2.0 * (mu - mean_ref[:, cols])
        psend[j] = p.astype(BF16).reshape(nl, own_rows, BLOCK)
        each(nl, s, lambda k, q: pu_copy(j, k, q).start())
        pall[s, j] = psend[j, s]

    def slopes(j):
        cols = slice(j * BLOCK, (j + 1) * BLOCK)

        def layer(l, carry):
            scale = ss[l, 0:1, cols]
            half = zall[l, j, pl.ds(pl.multiple_of(s * own_rows, own_rows), own_rows), :] * scale + ss[l, 1:2, cols]
            t = jnp.tanh(half)
            slope[l, j] = (1.0 + t) * (1.0 + half * (1.0 - t)) * scale
            return carry
        lax.fori_loop(0, nl, layer, 0)

    def backward(j):
        cols = slice(j * BLOCK, (j + 1) * BLOCK)

        def layer(i, up):
            l = nl - 1 - i

            @pl.when(l != s)
            def _():
                d = pall.at[l, j]
                copy(d, d, pu_s.at[j, 0], pu_r.at[j, l], l, b).wait_recv()
            grad = (up * slope[l, j] + pall[l, j].astype(F32)).astype(BF16)
            w = wall[l, j].reshape(BLOCK, GROUP)
            parts = []
            for g in range(BLOCK // GROUP):
                part = slice(g * GROUP, (g + 1) * GROUP)
                parts.append(dot(grad[:, part], w[part], ((1,), (1,))))
            return jnp.concatenate(parts, axis=1).astype(BF16).astype(F32)
        up = lax.fori_loop(0, nl, layer, jnp.zeros((own_rows, BLOCK), F32))
        out_ref[:, cols] = up.astype(BF16)

    def loss_plane():
        def arrived(k, q):
            copy(lossb.at[q], lossb.at[q], lb_s.at[0], lb_r.at[q], s, q).wait_recv()
        each(nb, b, arrived)
        lossz[s] = jnp.sum(lossb[...], axis=0)
        each(nl, s, lambda k, q: lz_copy(k, q).start())

    def loss_all():
        def arrived(k, q):
            copy(lossz.at[q], lossz.at[q], lz_s.at[0], lz_r.at[q], q, b).wait_recv()
        each(nl, s, arrived)
        total = jnp.sum(jnp.sum(lossz[...], axis=0), axis=(0, 1), keepdims=True)
        loss_ref[...] = jnp.broadcast_to(total * (1.0 / (nl * nj * BLOCK)), loss_ref.shape)

    def early_sends():
        each(nl, s, lambda k, q: ss_copy(k, q).wait_send())

        def block_sends(j, carry):
            each(nl, s, lambda k, q: z_copy(j, k, q).wait_send())
            each(nb, b, lambda k, q: mu_copy(j, k, q).wait_send())
            each(nc, chip, lambda k, q: rs_copy(j, k, q).wait_send())
            each(nc, chip, lambda k, q: ag_copy(j, k, q).wait_send())
            zc_copy(j, core).wait_send()
            ex_copy(j, core).wait_send()

            def weight_sends(_, l):
                each(nc, chip, lambda k, q: w2_copy(l, j, k, q).wait_send())
                w3_copy(l, j, core).wait_send()
            each(nl, s, weight_sends)
            return carry
        lax.fori_loop(0, nj, block_sends, 0)

    lead = (spread_chips, spread_mate, forward, gram, reduce, swap, pull, slopes)
    order = []
    for t in range(nj + 5):
        for stage, delay in zip(lead, LAG):
            if 0 <= t - delay < nj:
                order.append((stage, t - delay))
    Z, M, F, C, E, X, Q, S, B = lead + (backward,)
    if nj == 3:
        order = [(Z, 0), (Z, 1), (M, 0), (F, 0), (Z, 2), (M, 1), (C, 0), (F, 1), (M, 2), (C, 1), (F, 2), (E, 0),
                 (C, 2), (X, 0), (E, 1), (Q, 0), (X, 1), (E, 2), (Q, 1), (S, 0), (S, 1), (S, 2), (B, 0),
                 (X, 2), (Q, 2)]
    else:
        order += [(B, 0)]
    for stage, j in order:
        stage(j)
    loss_plane()
    early_sends()
    for j in range(1, nj):
        backward(j)
    loss_all()
    each(nl, s, lambda k, q: lz_copy(k, q).wait_send())
    each(nb, b, lambda k, q: lb_copy(k, q).wait_send())
    for j in range(nj):
        each(nl, s, lambda k, q: pu_copy(j, k, q).wait_send())


def shards(nl, nb, images, weights, bn_mean, bn_var, bn_gain, bn_bias):
    rows, channels = images.shape[1:]
    nj = channels // BLOCK
    nc = nb // 2
    own_rows = rows // nl
    piece = GROUP // nc
    vmem, dma = pltpu.VMEM, pltpu.SemaphoreType.DMA
    halves = BLOCK // GROUP
    sems = []
    for shape in ((nj, nl), (nl,), (nl, nj, nc), (nl, nj), (nj,), (nj, nb), (nj, nc), (nj, nc),
                  (nj,), (nj, nl), (nb,), (nl,)):
        sems += [dma(shape), dma(shape)]
    out, loss = pl.pallas_call(
        functools.partial(kernel, nl, nb, nj),
        out_shape=(jax.ShapeDtypeStruct((own_rows, channels), BF16),
                   jax.ShapeDtypeStruct((8, 128), F32)),
        in_specs=[pl.BlockSpec(memory_space=vmem)] * 6,
        out_specs=(pl.BlockSpec(memory_space=vmem),) * 2,
        scratch_shapes=[
            vmem((nl, nj, nc, 2, BLOCK // nb, GROUP), BF16),
            vmem((nl, 2, channels), F32),
            vmem((rows, BLOCK), BF16),
            vmem((nl, nj, rows, BLOCK), F32),
            vmem((nl, nj, own_rows, BLOCK), F32),
            vmem((nj, 2, halves, rows, GROUP), BF16),
            vmem((nj, nc, piece, WIDE), F32),
            vmem((nj, nc, piece, WIDE), BF16),
            vmem((nj, nc, piece, WIDE), BF16),
            vmem((nj, 2, nc, piece, WIDE), BF16),
            vmem((nj, nl, own_rows, BLOCK), BF16),
            vmem((nl, nj, own_rows, BLOCK), BF16),
            vmem((nj, nb, 1, BLOCK), F32),
            vmem((1, BLOCK), F32),
            vmem((nb, 8, 128), F32),
            vmem((nl, 8, 128), F32),
        ] + sems,
        compiler_params=pltpu.CompilerParams(
            collective_id=0, has_side_effects=True, vmem_limit_bytes=60 * 1024 * 1024),
    )(images[0], weights.reshape(nj, nc, 2, BLOCK // nb, GROUP), bn_mean, bn_var, bn_gain, bn_bias)
    return (out[None], loss[0, 0])


def solution(mesh):
    placed = (
        P("batch", None, None),
        P("section", None, None, None),
        P("section", None),
        P("section", None),
        P("section", None),
        P("section", None),
    )
    return jax.shard_map(
        functools.partial(shards, mesh.shape["section"], mesh.shape["batch"]),
        mesh=mesh,
        in_specs=placed,
        out_specs=(P("batch", "section", None), P()),
        check_vma=False,
    )
```

```python
import functools

import jax
import jax.numpy as jnp
from jax import lax
from jax.experimental import pallas as pl
from jax.experimental.pallas import tpu as pltpu
from jax.sharding import PartitionSpec as P

BLOCK = 512
GROUP = 256
HALF = 128
WIDE = GROUP + HALF
EPS = 1e-05
MESH = pl.DeviceIdType.MESH
F32 = jnp.float32
BF16 = jnp.bfloat16


def dot(a, b, dims):
    return lax.dot_general(a, b, (dims, ((), ())), preferred_element_type=F32)


def kernel(nl, nb, nj, x_ref, w_ref, mean_ref, var_ref, gain_ref, bias_ref, out_ref, loss_ref,
           wall, ss, xbuf, zall, slope, zc, sacc, srs, rs, e, psend, pall, mub, mu_all, lossb, lossz,
           z_s, z_r, ss_s, ss_r, w2_s, w2_r, w3_s, w3_r, zc_s, zc_r, mu_s, mu_r, rs_s, rs_r,
           ag_s, ag_r, ex_s, ex_r, pu_s, pu_r, lb_s, lb_r, lz_s, lz_r):
    s = lax.axis_index("section")
    b = lax.axis_index("batch")
    chip, core = b // 2, b % 2
    nc = nb // 2
    mate = chip * 2 + (1 - core)
    rows = x_ref.shape[0]
    own_rows = rows // nl
    piece = GROUP // nc
    row_total = rows * nb

    def copy(src, dst, ssem, rsem, sec, bat):
        return pltpu.make_async_remote_copy(
            src_ref=src, dst_ref=dst, send_sem=ssem, recv_sem=rsem,
            device_id=(sec, bat), device_id_type=MESH)

    def each(count, me, body):
        def step(k, carry):
            body(k, lax.rem(me + k, count))
            return carry
        lax.fori_loop(1, count, step, 0)

    def z_copy(j, k, q):
        return copy(w_ref.at[j, chip, core], wall.at[s, j, chip, core], z_s.at[j, k], z_r.at[j, s], q, b)

    def z_wait(j, l):
        d = wall.at[l, j, chip, core]
        copy(d, d, z_s.at[j, 0], z_r.at[j, l], l, b).wait_recv()

    def ss_copy(k, q):
        return copy(ss.at[s], ss.at[s], ss_s.at[k], ss_r.at[s], q, b)

    def w2_copy(l, j, k, q):
        d = wall.at[l, j, chip, core]
        return copy(d, d, w2_s.at[l, j, k], w2_r.at[l, j, chip], s, q * 2 + core)

    def w3_copy(l, j, half):
        d = wall.at[l, j, :, half]
        return copy(d, d, w3_s.at[l, j], w3_r.at[l, j], s, mate)

    def zc_copy(j, half):
        return copy(zc.at[j, half], zc.at[j, half], zc_s.at[j], zc_r.at[j], s, mate)

    def mu_copy(j, k, q):
        return copy(mub.at[j, b], mub.at[j, b], mu_s.at[j, k], mu_r.at[j, b], s, q)

    def rs_copy(j, k, q):
        return copy(srs.at[j, q], rs.at[j, chip], rs_s.at[j, k], rs_r.at[j, chip], s, q * 2 + core)

    def ag_copy(j, k, q):
        d = e.at[j, core, chip]
        return copy(d, d, ag_s.at[j, k], ag_r.at[j, chip], s, q * 2 + core)

    def ex_copy(j, half):
        return copy(e.at[j, half], e.at[j, half], ex_s.at[j], ex_r.at[j], s, mate)

    def pu_copy(j, k, q):
        return copy(psend.at[j, q], pall.at[s, j], pu_s.at[j, k], pu_r.at[j, s], q, b)

    def lb_copy(k, q):
        return copy(lossb.at[b], lossb.at[b], lb_s.at[k], lb_r.at[b], s, q)

    def lz_copy(k, q):
        return copy(lossz.at[s], lossz.at[s], lz_s.at[k], lz_r.at[s], q, b)

    barrier = pltpu.get_barrier_semaphore()
    each(nb, b, lambda k, q: pl.semaphore_signal(barrier, inc=1, device_id=(s, q), device_id_type=MESH))
    each(nl, s, lambda k, q: pl.semaphore_signal(barrier, inc=1, device_id=(q, b), device_id_type=MESH))
    scale_own = gain_ref[...] * lax.rsqrt(var_ref[...] + EPS)
    ss[s, 0:1, :] = 0.5 * scale_own
    ss[s, 1:2, :] = 0.5 * (bias_ref[...] - mean_ref[...] * scale_own)
    for j in range(nj):
        wall[s, j] = w_ref[j]
    pl.semaphore_wait(barrier, nb - 1 + nl - 1)

    each(nl, s, lambda k, q: ss_copy(k, q).start())
    for j in range(nj):
        each(nl, s, lambda k, q: z_copy(j, k, q).start())

    def spread_chips(j):
        def one(_, l):
            z_wait(j, l)
            each(nc, chip, lambda k, q: w2_copy(l, j, k, q).start())
        each(nl, s, one)

    def spread_mate(j):
        def one(_, l):
            def arrived(k, q):
                d = wall.at[l, j, q, core]
                copy(d, d, w2_s.at[l, j, 0], w2_r.at[l, j, q], s, q * 2 + core).wait_recv()
            each(nc, chip, arrived)
            w3_copy(l, j, core).start()
        each(nl, s, one)

    def forward(j):
        cols = slice(j * BLOCK, (j + 1) * BLOCK)
        xbuf[...] = x_ref[:, cols]

        def layer(l, carry):
            @pl.when(l != s)
            def _():
                w3_copy(l, j, 1 - core).wait_recv()
                if j == 0:
                    copy(ss.at[l], ss.at[l], ss_s.at[0], ss_r.at[l], l, b).wait_recv()
            w = wall[l, j].reshape(BLOCK, GROUP)
            for g in range(BLOCK // GROUP):
                part = slice(g * GROUP, (g + 1) * GROUP)
                lanes = slice(j * BLOCK + g * GROUP, j * BLOCK + (g + 1) * GROUP)
                z = dot(xbuf[:, part], w[part], ((1,), (0,)))
                zall[l, j, :, part] = z
                half = z * ss[l, 0:1, lanes] + ss[l, 1:2, lanes]
                xbuf[:, part] = (half + half * jnp.tanh(half)).astype(BF16)
            return carry
        lax.fori_loop(0, nl, layer, 0)
        z = zall[s, j]
        mu = jnp.sum(z, axis=0, keepdims=True) * (1.0 / rows)
        mub[j, b] = mu
        each(nb, b, lambda k, q: mu_copy(j, k, q).start())
        centered = (z - mu).astype(BF16)
        for h in range(BLOCK // GROUP):
            zc[j, core, h] = centered[:, h * GROUP:(h + 1) * GROUP]
        zc_copy(j, core).start()

    def gram(j):
        zc_copy(j, 1 - core).wait_recv()
        cross = pl.ds(pl.multiple_of(core * HALF, HALF), HALF)
        square = dot(zc[j, 0, core], zc[j, 0, core], ((0,), (0,))) + dot(
            zc[j, 1, core], zc[j, 1, core], ((0,), (0,)))
        other = dot(zc[j, 0, 0], zc[j, 0, 1, :, cross], ((0,), (0,))) + dot(
            zc[j, 1, 0], zc[j, 1, 1, :, cross], ((0,), (0,)))
        total = jnp.concatenate([square, other], axis=1).reshape(nc, piece, WIDE)
        sacc[j] = total
        srs[j] = total.astype(BF16)
        each(nc, chip, lambda k, q: rs_copy(j, k, q).start())

    def batch_mean(j):
        return jnp.sum(mub[j], axis=0) * (1.0 / nb)

    def reduce(j):
        cols = slice(j * BLOCK, (j + 1) * BLOCK)

        def arrived_mu(k, q):
            copy(mub.at[j, q], mub.at[j, q], mu_s.at[j, 0], mu_r.at[j, q], s, q).wait_recv()
        each(nb, b, arrived_mu)
        mu = batch_mean(j)
        mine = pl.ds(pl.multiple_of(core * GROUP, GROUP), GROUP)
        cross = pl.ds(pl.multiple_of(GROUP + core * HALF, HALF), HALF)
        var_lanes = pl.ds(pl.multiple_of(j * BLOCK + core * GROUP, GROUP), GROUP)
        mu_all[...] = mu
        mu_mine, mu_cross, mu_low = mu_all[:, mine], mu_all[:, cross], mu[:, :GROUP]
        eye = (lax.broadcasted_iota(jnp.int32, (piece, GROUP), 0) + chip * piece
               == lax.broadcasted_iota(jnp.int32, (piece, GROUP), 1)).astype(F32)

        def between(i, acc):
            low = mub[j, i, :, :GROUP] - mu_low
            d_mine = mub[j, i, :, mine] - mu_mine
            d_cross = mub[j, i, :, cross] - mu_cross
            column = jnp.sum(eye * d_mine, axis=1, keepdims=True)
            column_low = jnp.sum(eye * low, axis=1, keepdims=True)
            return (acc[0] + column * d_mine, acc[1] + column_low * d_cross)
        corr = jnp.concatenate(lax.fori_loop(
            0, nb, between, (jnp.zeros((piece, GROUP), F32), jnp.zeros((piece, HALF), F32))), axis=1)
        sacc[j, chip] = sacc[j, chip] + corr * rows

        def arrived(k, q):
            copy(rs.at[j, q], rs.at[j, q], rs_s.at[j, 0], rs_r.at[j, q], s, q * 2 + core).wait_recv()
            sacc[j, chip] = sacc[j, chip] + rs[j, q].astype(F32)
        each(nc, chip, arrived)
        cov = sacc[j, chip] * (1.0 / row_total)
        dev, dev_cross = cov[:, :GROUP] - eye * var_ref[:, var_lanes], cov[:, GROUP:]
        e[j, core, chip] = jnp.concatenate([dev, dev_cross], axis=1).astype(BF16)
        each(nc, chip, lambda k, q: ag_copy(j, k, q).start())
        square = jnp.sum((dev * dev).reshape(piece // 8, 8, GROUP), axis=0) * 0.25
        double = jnp.sum((dev_cross * dev_cross).reshape(piece // 8, 8, HALF), axis=0) * 0.5
        off = mu - mean_ref[:, cols]
        off = off * off
        off = sum(off[:, i * HALF:(i + 1) * HALF] for i in range(BLOCK // HALF))
        head = (lax.broadcasted_iota(jnp.int32, (8, HALF), 0) + b == 0).astype(F32)
        tile = square[:, :HALF] + square[:, HALF:] + double + head * off
        if j == 0:
            lossb[b] = tile
        else:
            lossb[b] = lossb[b] + tile
        if j == nj - 1:
            each(nb, b, lambda k, q: lb_copy(k, q).start())

    def swap(j):
        def arrived(k, q):
            d = e.at[j, core, q]
            copy(d, d, ag_s.at[j, 0], ag_r.at[j, q], s, q * 2 + core).wait_recv()
        each(nc, chip, arrived)
        ex_copy(j, core).start()

    def pull(j):
        cols = slice(j * BLOCK, (j + 1) * BLOCK)
        mu = batch_mean(j)
        ex_copy(j, 1 - core).wait_recv()
        c0 = (zall[s, j, :, :GROUP] - mu[:, :GROUP]).astype(BF16)
        c1 = (zall[s, j, :, GROUP:] - mu[:, GROUP:]).astype(BF16)
        e0, e1 = e[j, 0].reshape(GROUP, WIDE), e[j, 1].reshape(GROUP, WIDE)
        cross = jnp.concatenate([e0[:, GROUP:], e1[:, GROUP:]], axis=1)
        p0 = dot(c0, e0[:, :GROUP], ((1,), (0,))) + dot(c1, cross, ((1,), (1,)))
        p1 = dot(c0, cross, ((1,), (0,))) + dot(c1, e1[:, :GROUP], ((1,), (0,)))
        p = jnp.concatenate([p0, p1], axis=1) + 2.0 * (mu - mean_ref[:, cols])
        psend[j] = p.astype(BF16).reshape(nl, own_rows, BLOCK)
        each(nl, s, lambda k, q: pu_copy(j, k, q).start())
        pall[s, j] = psend[j, s]

    def slopes(j):
        cols = slice(j * BLOCK, (j + 1) * BLOCK)

        def layer(l, carry):
            scale = ss[l, 0:1, cols]
            half = zall[l, j, pl.ds(pl.multiple_of(s * own_rows, own_rows), own_rows), :] * scale + ss[l, 1:2, cols]
            t = jnp.tanh(half)
            slope[l, j] = (1.0 + t) * (1.0 + half * (1.0 - t)) * scale
            return carry
        lax.fori_loop(0, nl, layer, 0)

    def backward(j):
        cols = slice(j * BLOCK, (j + 1) * BLOCK)

        def layer(i, up):
            l = nl - 1 - i

            @pl.when(l != s)
            def _():
                d = pall.at[l, j]
                copy(d, d, pu_s.at[j, 0], pu_r.at[j, l], l, b).wait_recv()
            grad = (up * slope[l, j] + pall[l, j].astype(F32)).astype(BF16)
            w = wall[l, j].reshape(BLOCK, GROUP)
            parts = []
            for g in range(BLOCK // GROUP):
                part = slice(g * GROUP, (g + 1) * GROUP)
                parts.append(dot(grad[:, part], w[part], ((1,), (1,))))
            return jnp.concatenate(parts, axis=1).astype(BF16).astype(F32)
        up = lax.fori_loop(0, nl, layer, jnp.zeros((own_rows, BLOCK), F32))
        out_ref[:, cols] = up.astype(BF16)

    def loss_plane():
        def arrived(k, q):
            copy(lossb.at[q], lossb.at[q], lb_s.at[0], lb_r.at[q], s, q).wait_recv()
        each(nb, b, arrived)
        lossz[s] = jnp.sum(lossb[...], axis=0)
        each(nl, s, lambda k, q: lz_copy(k, q).start())

    def loss_all():
        def arrived(k, q):
            copy(lossz.at[q], lossz.at[q], lz_s.at[0], lz_r.at[q], q, b).wait_recv()
        each(nl, s, arrived)
        loss_ref[0, 0] = jnp.sum(jnp.sum(lossz[...], axis=0)) * (1.0 / (nl * nj * BLOCK))

    def early_sends():
        each(nl, s, lambda k, q: ss_copy(k, q).wait_send())

        def block_sends(j, carry):
            each(nl, s, lambda k, q: z_copy(j, k, q).wait_send())
            each(nb, b, lambda k, q: mu_copy(j, k, q).wait_send())
            each(nc, chip, lambda k, q: rs_copy(j, k, q).wait_send())
            each(nc, chip, lambda k, q: ag_copy(j, k, q).wait_send())
            zc_copy(j, core).wait_send()
            ex_copy(j, core).wait_send()

            def weight_sends(_, l):
                each(nc, chip, lambda k, q: w2_copy(l, j, k, q).wait_send())
                w3_copy(l, j, core).wait_send()
            each(nl, s, weight_sends)
            return carry
        lax.fori_loop(0, nj, block_sends, 0)

    Z, M, F, C, E, X, Q, S, B = (
        spread_chips, spread_mate, forward, gram, reduce, swap, pull, slopes, backward)
    order = [(Z, 0), (M, 0), (F, 0), (Z, 1), (C, 0), (M, 1), (F, 1), (E, 0), (Z, 2), (C, 1), (X, 0), (Q, 0),
             (M, 2), (F, 2), (E, 1), (C, 2), (X, 1), (Q, 1), (E, 2), (S, 0), (S, 1), (S, 2), (B, 0), (X, 2), (Q, 2)]
    for stage, j in order:
        stage(j)
    loss_plane()
    early_sends()
    for j in range(1, nj):
        backward(j)
    loss_all()
    each(nl, s, lambda k, q: lz_copy(k, q).wait_send())
    each(nb, b, lambda k, q: lb_copy(k, q).wait_send())
    for j in range(nj):
        each(nl, s, lambda k, q: pu_copy(j, k, q).wait_send())


def shards(nl, nb, images, weights, bn_mean, bn_var, bn_gain, bn_bias):
    rows, channels = images.shape[1:]
    nj = channels // BLOCK
    nc = nb // 2
    own_rows = rows // nl
    piece = GROUP // nc
    vmem, dma = pltpu.VMEM, pltpu.SemaphoreType.DMA
    halves = BLOCK // GROUP
    sems = []
    for shape in ((nj, nl), (nl,), (nl, nj, nc), (nl, nj), (nj,), (nj, nb), (nj, nc), (nj, nc),
                  (nj,), (nj, nl), (nb,), (nl,)):
        sems += [dma(shape), dma(shape)]
    out, loss = pl.pallas_call(
        functools.partial(kernel, nl, nb, nj),
        out_shape=(jax.ShapeDtypeStruct((own_rows, channels), BF16),
                   jax.ShapeDtypeStruct((1, 1), F32)),
        in_specs=[pl.BlockSpec(memory_space=vmem)] * 6,
        out_specs=(pl.BlockSpec(memory_space=vmem), pl.BlockSpec(memory_space=pltpu.SMEM)),
        scratch_shapes=[
            vmem((nl, nj, nc, 2, BLOCK // nb, GROUP), BF16),
            vmem((nl, 2, channels), F32),
            vmem((rows, BLOCK), BF16),
            vmem((nl, nj, rows, BLOCK), F32),
            vmem((nl, nj, own_rows, BLOCK), F32),
            vmem((nj, 2, halves, rows, GROUP), BF16),
            vmem((nj, nc, piece, WIDE), F32),
            vmem((nj, nc, piece, WIDE), BF16),
            vmem((nj, nc, piece, WIDE), BF16),
            vmem((nj, 2, nc, piece, WIDE), BF16),
            vmem((nj, nl, own_rows, BLOCK), BF16),
            vmem((nl, nj, own_rows, BLOCK), BF16),
            vmem((nj, nb, 1, BLOCK), F32),
            vmem((1, BLOCK), F32),
            vmem((nb, 8, 128), F32),
            vmem((nl, 8, 128), F32),
        ] + sems,
        compiler_params=pltpu.CompilerParams(
            collective_id=0, has_side_effects=True, vmem_limit_bytes=60 * 1024 * 1024),
    )(images[0], weights.reshape(nj, nc, 2, BLOCK // nb, GROUP), bn_mean, bn_var, bn_gain, bn_bias)
    return (out[None], loss.reshape(()))


def solution(mesh):
    placed = (
        P("batch", None, None),
        P("section", None, None, None),
        P("section", None),
        P("section", None),
        P("section", None),
        P("section", None),
    )
    return jax.shard_map(
        functools.partial(shards, mesh.shape["section"], mesh.shape["batch"]),
        mesh=mesh,
        in_specs=placed,
        out_specs=(P("batch", "section", None), P()),
        check_vma=False,
    )
```

```python
import functools

import jax
import jax.numpy as jnp
from jax import lax
from jax.experimental import pallas as pl
from jax.experimental.pallas import tpu as pltpu
from jax.sharding import PartitionSpec as P

BLOCK = 512
GROUP = 256
HALF = 128
WIDE = GROUP + HALF
EPS = 1e-05
MESH = pl.DeviceIdType.MESH
F32 = jnp.float32
BF16 = jnp.bfloat16


def dot(a, b, dims):
    return lax.dot_general(a, b, (dims, ((), ())), preferred_element_type=F32)


def kernel(nl, nb, nj, x_ref, w_ref, mean_ref, var_ref, gain_ref, bias_ref, out_ref, loss_ref,
           wall, ss, xbuf, zall, slope, zc, sacc, srs, rs, e, psend, pall, mub, mu_all, lossb, lossz,
           send, recv):
    s = lax.axis_index("section")
    b = lax.axis_index("batch")
    chip, core = b // 2, b % 2
    nc = nb // 2
    mate = chip * 2 + (1 - core)
    rows = x_ref.shape[0]
    own_rows = rows // nl
    piece = GROUP // nc
    row_total = rows * nb

    def copy(src, dst, ssem, rsem, sec, bat):
        return pltpu.make_async_remote_copy(
            src_ref=src, dst_ref=dst, send_sem=ssem, recv_sem=rsem,
            device_id=(sec, bat), device_id_type=MESH)

    def each(count, me, body):
        if count <= 8:
            for k in range(1, count):
                body(k, lax.rem(me + k, count))
        else:
            def step(k, carry):
                body(k, lax.rem(me + k, count))
                return carry
            lax.fori_loop(1, count, step, 0)

    def loop(count, body, carry):
        if count > 8:
            return lax.fori_loop(0, count, body, carry)
        for i in range(count):
            carry = body(i, carry)
        return carry

    def slot(l):
        return lax.rem(l - s + nl, nl)

    SS, WZ, WC, WM, ZC, MM, MC, RS, AG, EX, PU, LB, LZ = range(13)

    def got(kind, j, ref):
        copy(ref, ref, send.at[kind], recv.at[kind, j], s, mate).wait_recv()

    def sent(kind, ref):
        copy(ref, ref, send.at[kind], recv.at[kind, 0], s, mate).wait_send()

    def put(kind, j, src, dst, sec, bat):
        copy(src, dst, send.at[kind], recv.at[kind, j], sec, bat).start()

    barrier = pltpu.get_barrier_semaphore()
    each(nb, b, lambda k, q: pl.semaphore_signal(barrier, inc=1, device_id=(s, q), device_id_type=MESH))
    each(nl, s, lambda k, q: pl.semaphore_signal(barrier, inc=1, device_id=(q, b), device_id_type=MESH))
    scale_own = gain_ref[...] * lax.rsqrt(var_ref[...] + EPS)
    ss[0, 0:1, :] = 0.5 * scale_own
    ss[0, 1:2, :] = 0.5 * (bias_ref[...] - mean_ref[...] * scale_own)
    for j in range(nj):
        wall[0, j] = w_ref[j]
    pl.semaphore_wait(barrier, nb - 1 + nl - 1)

    each(nl, s, lambda k, q: put(SS, 0, ss.at[0], ss.at[nl - k], q, b))
    for j in range(nj):
        each(nl, s, lambda k, q: put(WZ, j, w_ref.at[j, chip, core], wall.at[nl - k, j, chip, core], q, b))

    def spread_chips(j):
        mine = wall.at[pl.ds(1, nl - 1), j, chip, core]
        got(WZ, j, mine)
        each(nc, chip, lambda k, q: put(WC, j, mine, mine, s, q * 2 + core))

    def spread_mate(j):
        got(WC, j, wall.at[pl.ds(1, nl - 1), j, pl.ds(1, nc - 1), core])
        mine = wall.at[pl.ds(1, nl - 1), j, :, core]
        put(WM, j, mine, mine, s, mate)

    def forward(j):
        cols = slice(j * BLOCK, (j + 1) * BLOCK)
        got(WM, j, wall.at[pl.ds(1, nl - 1), j, :, 1 - core])
        if j == 0:
            got(SS, 0, ss.at[pl.ds(1, nl - 1)])
        xbuf[...] = x_ref[:, cols]

        def layer(l, carry):
            at = slot(l)
            w = wall[at, j].reshape(BLOCK, GROUP)
            for g in range(BLOCK // GROUP):
                part = slice(g * GROUP, (g + 1) * GROUP)
                lanes = slice(j * BLOCK + g * GROUP, j * BLOCK + (g + 1) * GROUP)
                z = dot(xbuf[:, part], w[part], ((1,), (0,)))
                zall[l, j, :, part] = z
                half = z * ss[at, 0:1, lanes] + ss[at, 1:2, lanes]
                xbuf[:, part] = (half + half * jnp.tanh(half)).astype(BF16)
            return carry
        loop(nl, layer, 0)
        z = zall[s, j]
        mu = jnp.sum(z, axis=0, keepdims=True) * (1.0 / rows)
        mub[j, chip, core] = mu
        put(MM, j, mub.at[j, chip, core], mub.at[j, chip, core], s, mate)
        centered = (z - mu).astype(BF16)
        for h in range(BLOCK // GROUP):
            zc[j, core, h] = centered[:, h * GROUP:(h + 1) * GROUP]
        put(ZC, j, zc.at[j, core], zc.at[j, core], s, mate)

    def gram(j):
        got(MM, j, mub.at[j, chip, 1 - core])
        each(nc, chip, lambda k, q: put(MC, j, mub.at[j, chip], mub.at[j, chip], s, q * 2 + core))
        got(ZC, j, zc.at[j, 1 - core])
        cross = pl.ds(pl.multiple_of(core * HALF, HALF), HALF)
        square = dot(zc[j, 0, core], zc[j, 0, core], ((0,), (0,))) + dot(
            zc[j, 1, core], zc[j, 1, core], ((0,), (0,)))
        other = dot(zc[j, 0, 0], zc[j, 0, 1, :, cross], ((0,), (0,))) + dot(
            zc[j, 1, 0], zc[j, 1, 1, :, cross], ((0,), (0,)))
        total = jnp.concatenate([square, other], axis=1).reshape(nc, piece, WIDE)
        sacc[j] = total
        srs[j] = total.astype(BF16)
        each(nc, chip, lambda k, q: put(RS, j, srs.at[j, q], rs.at[j, nc - k], s, q * 2 + core))

    def batch_mean(j):
        return jnp.sum(mub[j], axis=(0, 1)) * (1.0 / nb)

    def reduce(j):
        cols = slice(j * BLOCK, (j + 1) * BLOCK)

        got(MC, j, mub.at[j, pl.ds(1, nc - 1)])
        mu = batch_mean(j)
        mine = pl.ds(pl.multiple_of(core * GROUP, GROUP), GROUP)
        cross = pl.ds(pl.multiple_of(GROUP + core * HALF, HALF), HALF)
        var_lanes = pl.ds(pl.multiple_of(j * BLOCK + core * GROUP, GROUP), GROUP)
        mu_all[...] = mu
        mu_mine, mu_cross, mu_low = mu_all[:, mine], mu_all[:, cross], mu[:, :GROUP]
        eye = (lax.broadcasted_iota(jnp.int32, (piece, GROUP), 0) + chip * piece
               == lax.broadcasted_iota(jnp.int32, (piece, GROUP), 1)).astype(F32)

        def between(i, acc):
            low = mub[j, i // 2, i % 2, :, :GROUP] - mu_low
            d_mine = mub[j, i // 2, i % 2, :, mine] - mu_mine
            d_cross = mub[j, i // 2, i % 2, :, cross] - mu_cross
            column = jnp.sum(eye * d_mine, axis=1, keepdims=True)
            column_low = jnp.sum(eye * low, axis=1, keepdims=True)
            return (acc[0] + column * d_mine, acc[1] + column_low * d_cross)
        corr = jnp.concatenate(loop(
            nb, between, (jnp.zeros((piece, GROUP), F32), jnp.zeros((piece, HALF), F32))), axis=1)
        cov = sacc[j, chip] + corr * rows
        got(RS, j, rs.at[j, pl.ds(1, nc - 1)])
        cov = loop(nc - 1, lambda i, acc: acc + rs[j, i + 1].astype(F32), cov) * (1.0 / row_total)
        dev, dev_cross = cov[:, :GROUP] - eye * var_ref[:, var_lanes], cov[:, GROUP:]
        e[j, core, chip] = jnp.concatenate([dev, dev_cross], axis=1).astype(BF16)
        own = e.at[j, core, chip]
        each(nc, chip, lambda k, q: put(AG, j, own, own, s, q * 2 + core))
        square = jnp.sum((dev * dev).reshape(piece // 8, 8, GROUP), axis=0) * 0.25
        double = jnp.sum((dev_cross * dev_cross).reshape(piece // 8, 8, HALF), axis=0) * 0.5
        off = mu - mean_ref[:, cols]
        off = off * off
        off = sum(off[:, i * HALF:(i + 1) * HALF] for i in range(BLOCK // HALF))
        head = (lax.broadcasted_iota(jnp.int32, (8, HALF), 0) + b == 0).astype(F32)
        tile = square[:, :HALF] + square[:, HALF:] + double + head * off
        if j == 0:
            lossb[0] = tile
        else:
            lossb[0] = lossb[0] + tile
        if j == nj - 1:
            each(nb, b, lambda k, q: put(LB, 0, lossb.at[0], lossb.at[nb - k], s, q))

    def swap(j):
        got(AG, j, e.at[j, core, pl.ds(1, nc - 1)])
        put(EX, j, e.at[j, core], e.at[j, core], s, mate)

    def pull(j):
        cols = slice(j * BLOCK, (j + 1) * BLOCK)
        mu = batch_mean(j)
        got(EX, j, e.at[j, 1 - core])
        c0 = (zall[s, j, :, :GROUP] - mu[:, :GROUP]).astype(BF16)
        c1 = (zall[s, j, :, GROUP:] - mu[:, GROUP:]).astype(BF16)
        e0, e1 = e[j, 0].reshape(GROUP, WIDE), e[j, 1].reshape(GROUP, WIDE)
        cross = jnp.concatenate([e0[:, GROUP:], e1[:, GROUP:]], axis=1)
        p0 = dot(c0, e0[:, :GROUP], ((1,), (0,))) + dot(c1, cross, ((1,), (1,)))
        p1 = dot(c0, cross, ((1,), (0,))) + dot(c1, e1[:, :GROUP], ((1,), (0,)))
        p = jnp.concatenate([p0, p1], axis=1) + 2.0 * (mu - mean_ref[:, cols])
        psend[j] = p.astype(BF16).reshape(nl, own_rows, BLOCK)
        each(nl, s, lambda k, q: put(PU, j, psend.at[j, q], pall.at[nl - k, j], q, b))
        pall[0, j] = psend[j, s]

    def slopes(j):
        cols = slice(j * BLOCK, (j + 1) * BLOCK)

        def layer(l, carry):
            at = slot(l)
            scale = ss[at, 0:1, cols]
            half = zall[l, j, pl.ds(pl.multiple_of(s * own_rows, own_rows), own_rows), :] * scale + ss[at, 1:2, cols]
            t = jnp.tanh(half)
            slope[l, j] = (1.0 + t) * (1.0 + half * (1.0 - t)) * scale
            return carry
        loop(nl, layer, 0)

    def backward(j):
        cols = slice(j * BLOCK, (j + 1) * BLOCK)

        got(PU, j, pall.at[pl.ds(1, nl - 1), j])

        def layer(i, up):
            l = nl - 1 - i
            at = slot(l)
            grad = (up * slope[l, j] + pall[at, j].astype(F32)).astype(BF16)
            w = wall[at, j].reshape(BLOCK, GROUP)
            parts = []
            for g in range(BLOCK // GROUP):
                part = slice(g * GROUP, (g + 1) * GROUP)
                parts.append(dot(grad[:, part], w[part], ((1,), (1,))))
            return jnp.concatenate(parts, axis=1).astype(BF16).astype(F32)
        up = loop(nl, layer, jnp.zeros((own_rows, BLOCK), F32))
        out_ref[:, cols] = up.astype(BF16)

    def loss_plane():
        got(LB, 0, lossb.at[pl.ds(1, nb - 1)])
        lossz[0] = jnp.sum(lossb[...], axis=0)
        each(nl, s, lambda k, q: put(LZ, 0, lossz.at[0], lossz.at[nl - k], q, b))

    def loss_all():
        got(LZ, 0, lossz.at[pl.ds(1, nl - 1)])
        loss_ref[0, 0] = jnp.sum(jnp.sum(lossz[...], axis=0)) * (1.0 / (nl * nj * BLOCK))

    def early_sends():
        sent(SS, ss.at[pl.ds(1, nl - 1)])
        sent(WZ, wall.at[pl.ds(1, nl - 1), :, chip, core])
        sent(WC, wall.at[pl.ds(1, nl - 1), :, pl.ds(1, nc - 1), core])
        sent(WM, wall.at[pl.ds(1, nl - 1), :, :, core])
        sent(ZC, zc.at[:, core])
        sent(MM, mub.at[:, chip, core])
        sent(MC, mub.at[:, pl.ds(1, nc - 1)])
        sent(RS, srs.at[:, pl.ds(1, nc - 1)])
        sent(AG, e.at[:, core, pl.ds(1, nc - 1)])
        sent(EX, e.at[:, core])

    Z, M, F, C, E, X, Q, S, B = (
        spread_chips, spread_mate, forward, gram, reduce, swap, pull, slopes, backward)
    order = [(Z, 0), (Z, 1), (Z, 2), (M, 0), (F, 0), (M, 1), (C, 0), (F, 1), (M, 2), (C, 1), (F, 2), (E, 0),
             (C, 2), (X, 0), (E, 1), (Q, 0), (X, 1), (E, 2), (Q, 1), (S, 0), (S, 1), (S, 2), (B, 0), (X, 2), (Q, 2)]
    for stage, j in order:
        stage(j)
    loss_plane()
    early_sends()
    for j in range(1, nj):
        backward(j)
    loss_all()
    sent(LZ, lossz.at[pl.ds(1, nl - 1)])
    sent(LB, lossb.at[pl.ds(1, nb - 1)])
    sent(PU, psend.at[:, pl.ds(1, nl - 1)])


def shards(nl, nb, images, weights, bn_mean, bn_var, bn_gain, bn_bias):
    rows, channels = images.shape[1:]
    nj = channels // BLOCK
    nc = nb // 2
    own_rows = rows // nl
    piece = GROUP // nc
    vmem, dma = pltpu.VMEM, pltpu.SemaphoreType.DMA
    halves = BLOCK // GROUP
    out, loss = pl.pallas_call(
        functools.partial(kernel, nl, nb, nj),
        out_shape=(jax.ShapeDtypeStruct((own_rows, channels), BF16),
                   jax.ShapeDtypeStruct((1, 1), F32)),
        in_specs=[pl.BlockSpec(memory_space=vmem)] * 6,
        out_specs=(pl.BlockSpec(memory_space=vmem), pl.BlockSpec(memory_space=pltpu.SMEM)),
        scratch_shapes=[
            vmem((nl, nj, nc, 2, BLOCK // nb, GROUP), BF16),
            vmem((nl, 2, channels), F32),
            vmem((rows, BLOCK), BF16),
            vmem((nl, nj, rows, BLOCK), F32),
            vmem((nl, nj, own_rows, BLOCK), F32),
            vmem((nj, 2, halves, rows, GROUP), BF16),
            vmem((nj, nc, piece, WIDE), F32),
            vmem((nj, nc, piece, WIDE), BF16),
            vmem((nj, nc, piece, WIDE), BF16),
            vmem((nj, 2, nc, piece, WIDE), BF16),
            vmem((nj, nl, own_rows, BLOCK), BF16),
            vmem((nl, nj, own_rows, BLOCK), BF16),
            vmem((nj, nc, 2, 1, BLOCK), F32),
            vmem((1, BLOCK), F32),
            vmem((nb, 8, 128), F32),
            vmem((nl, 8, 128), F32),
            dma((13,)),
            dma((13, nj)),
        ],
        compiler_params=pltpu.CompilerParams(
            collective_id=0, has_side_effects=True, vmem_limit_bytes=60 * 1024 * 1024),
    )(images[0], weights.reshape(nj, nc, 2, BLOCK // nb, GROUP), bn_mean, bn_var, bn_gain, bn_bias)
    return (out[None], loss.reshape(()))


def solution(mesh):
    placed = (
        P("batch", None, None),
        P("section", None, None, None),
        P("section", None),
        P("section", None),
        P("section", None),
        P("section", None),
    )
    return jax.shard_map(
        functools.partial(shards, mesh.shape["section"], mesh.shape["batch"]),
        mesh=mesh,
        in_specs=placed,
        out_specs=(P("batch", "section", None), P()),
        check_vma=False,
    )
```

```python
import functools

import jax
import jax.numpy as jnp
from jax import lax
from jax.experimental import pallas as pl
from jax.experimental.pallas import tpu as pltpu
from jax.sharding import PartitionSpec as P

BLOCK = 512
GROUP = 256
HALF = 128
WIDE = GROUP + HALF
EPS = 1e-05
MESH = pl.DeviceIdType.MESH
F32 = jnp.float32
BF16 = jnp.bfloat16


def dot(a, b, dims):
    return lax.dot_general(a, b, (dims, ((), ())), preferred_element_type=F32)


def kernel(nl, nb, nj, x_ref, w_ref, mean_ref, var_ref, gain_ref, bias_ref, out_ref, loss_ref,
           wall, pp, ppo, xbuf, zall, slope, zc, sacc, srs, rs, e, pall, gout, outv, mub, mu_all, lossb, lossz, lossw,
           send, recv):
    s = lax.axis_index("section")
    b = lax.axis_index("batch")
    chip, core = b // 2, b % 2
    nc = nb // 2
    mate = chip * 2 + (1 - core)
    rows = x_ref.shape[0]
    own_rows = rows // nl
    piece = GROUP // nc
    row_total = rows * nb

    def copy(src, dst, ssem, rsem, sec, bat):
        return pltpu.make_async_remote_copy(
            src_ref=src, dst_ref=dst, send_sem=ssem, recv_sem=rsem,
            device_id=(sec, bat), device_id_type=MESH)

    def each(count, me, body):
        if count <= 8:
            for k in range(1, count):
                body(k, lax.rem(me + k, count))
        else:
            def step(k, carry):
                body(k, lax.rem(me + k, count))
                return carry
            lax.fori_loop(1, count, step, 0)

    def loop(count, body, carry):
        if count > 8:
            return lax.fori_loop(0, count, body, carry)
        for i in range(count):
            carry = body(i, carry)
        return carry

    def slot(l):
        return lax.rem(l - s + nl, nl)

    WZ, PP, WC, WM, ZC, MM, MC, RS, AG, EX, GO, LB, LZ = range(13)
    block = jnp.minimum(s, nj - 1)

    def got(kind, j, ref):
        copy(ref, ref, send.at[kind, 0], recv.at[kind, j], s, mate).wait_recv()

    def sent(kind, ref, j=0):
        copy(ref, ref, send.at[kind, j], recv.at[kind, 0], s, mate).wait_send()

    def put(kind, j, src, dst, sec, bat, out=0):
        copy(src, dst, send.at[kind, out], recv.at[kind, j], sec, bat).start()

    def planes(body):
        for j in range(nj):
            pl.when(j != s)(functools.partial(body, j))

    barrier = pltpu.get_barrier_semaphore()
    each(nb, b, lambda k, q: pl.semaphore_signal(barrier, inc=1, device_id=(s, q), device_id_type=MESH))
    each(nl, s, lambda k, q: pl.semaphore_signal(barrier, inc=1, device_id=(q, b), device_id_type=MESH))
    scale_own = gain_ref[...] * lax.rsqrt(var_ref[...] + EPS)
    shift_own = bias_ref[...] - mean_ref[...] * scale_own
    for j in range(nj):
        cols = slice(j * BLOCK, (j + 1) * BLOCK)
        ppo[j, 0:1, :] = 0.5 * scale_own[:, cols]
        ppo[j, 1:2, :] = 0.5 * shift_own[:, cols]
        ppo[j, 2:3, :] = mean_ref[:, cols]
        ppo[j, 3:4, :] = var_ref[:, cols]
    pp[0] = ppo[block]
    wall[0] = w_ref[block]
    pl.semaphore_wait(barrier, nb - 1 + nl - 1)

    def send_layer(j):
        at = lax.rem(s - j + nl, nl)
        put(WZ, 0, w_ref.at[j, chip, core], wall.at[at, chip, core], j, b, j)
        put(PP, 0, ppo.at[j], pp.at[at], j, b, j)
    planes(send_layer)

    def gather_weights():
        mine = wall.at[pl.ds(1, nl - 1), chip, core]
        got(WZ, 0, mine)
        each(nc, chip, lambda k, q: put(WC, 0, mine, mine, s, q * 2 + core))
        got(PP, 0, pp.at[pl.ds(1, nl - 1)])
        xbuf[...] = x_ref[:, pl.ds(pl.multiple_of(block * BLOCK, BLOCK), BLOCK)]
        got(WC, 0, wall.at[pl.ds(1, nl - 1), pl.ds(1, nc - 1), core])
        mine = wall.at[pl.ds(1, nl - 1), :, core]
        put(WM, 0, mine, mine, s, mate)
        got(WM, 0, wall.at[pl.ds(1, nl - 1), :, 1 - core])

    def forward(j):
        at = slot(j)
        w = wall[at].reshape(BLOCK, GROUP)
        for g in range(BLOCK // GROUP):
            part = slice(g * GROUP, (g + 1) * GROUP)
            z = dot(xbuf[:, part], w[part], ((1,), (0,)))
            zall[j, :, part] = z
            half = z * pp[at, 0:1, part] + pp[at, 1:2, part]
            xbuf[:, part] = (half + half * jnp.tanh(half)).astype(BF16)
        z = zall[j]
        mu = jnp.sum(z, axis=0, keepdims=True) * (1.0 / rows)
        mub[j, chip, core] = mu
        put(MM, j, mub.at[j, chip, core], mub.at[j, chip, core], s, mate)
        centered = (z - mu).astype(BF16)
        for h in range(BLOCK // GROUP):
            zc[j, core, h] = centered[:, h * GROUP:(h + 1) * GROUP]
        put(ZC, j, zc.at[j, core], zc.at[j, core], s, mate)

    def gram(j):
        got(MM, j, mub.at[j, chip, 1 - core])
        each(nc, chip, lambda k, q: put(MC, j, mub.at[j, chip], mub.at[j, chip], s, q * 2 + core))
        got(ZC, j, zc.at[j, 1 - core])
        cross = pl.ds(pl.multiple_of(core * HALF, HALF), HALF)
        square = dot(zc[j, 0, core], zc[j, 0, core], ((0,), (0,))) + dot(
            zc[j, 1, core], zc[j, 1, core], ((0,), (0,)))
        other = dot(zc[j, 0, 0], zc[j, 0, 1, :, cross], ((0,), (0,))) + dot(
            zc[j, 1, 0], zc[j, 1, 1, :, cross], ((0,), (0,)))
        total = jnp.concatenate([square, other], axis=1).reshape(nc, piece, WIDE)
        sacc[j] = total
        srs[j] = total.astype(BF16)
        each(nc, chip, lambda k, q: put(RS, j, srs.at[j, q], rs.at[j, nc - k], s, q * 2 + core))

    def batch_mean(j):
        return jnp.sum(mub[j], axis=(0, 1)) * (1.0 / nb)

    def reduce(j):
        at = slot(j)
        got(MC, j, mub.at[j, pl.ds(1, nc - 1)])
        mu = batch_mean(j)
        mine = pl.ds(pl.multiple_of(core * GROUP, GROUP), GROUP)
        cross = pl.ds(pl.multiple_of(GROUP + core * HALF, HALF), HALF)
        mu_all[...] = mu
        mu_mine, mu_cross, mu_low = mu_all[:, mine], mu_all[:, cross], mu[:, :GROUP]
        eye = (lax.broadcasted_iota(jnp.int32, (piece, GROUP), 0) + chip * piece
               == lax.broadcasted_iota(jnp.int32, (piece, GROUP), 1)).astype(F32)

        def between(i, acc):
            low = mub[j, i // 2, i % 2, :, :GROUP] - mu_low
            d_mine = mub[j, i // 2, i % 2, :, mine] - mu_mine
            d_cross = mub[j, i // 2, i % 2, :, cross] - mu_cross
            column = jnp.sum(eye * d_mine, axis=1, keepdims=True)
            column_low = jnp.sum(eye * low, axis=1, keepdims=True)
            return (acc[0] + column * d_mine, acc[1] + column_low * d_cross)
        corr = jnp.concatenate(loop(
            nb, between, (jnp.zeros((piece, GROUP), F32), jnp.zeros((piece, HALF), F32))), axis=1)
        cov = sacc[j, chip] + corr * rows
        got(RS, j, rs.at[j, pl.ds(1, nc - 1)])
        cov = loop(nc - 1, lambda i, acc: acc + rs[j, i + 1].astype(F32), cov) * (1.0 / row_total)
        dev, dev_cross = cov[:, :GROUP] - eye * pp[at, 3:4, mine], cov[:, GROUP:]
        e[j, core, chip] = jnp.concatenate([dev, dev_cross], axis=1).astype(BF16)
        own = e.at[j, core, chip]
        each(nc, chip, lambda k, q: put(AG, j, own, own, s, q * 2 + core))
        square = jnp.sum((dev * dev).reshape(piece // 8, 8, GROUP), axis=0) * 0.25
        double = jnp.sum((dev_cross * dev_cross).reshape(piece // 8, 8, HALF), axis=0) * 0.5
        off = mu - pp[at, 2:3, :]
        off = off * off
        off = sum(off[:, i * HALF:(i + 1) * HALF] for i in range(BLOCK // HALF))
        head = (lax.broadcasted_iota(jnp.int32, (8, HALF), 0) + b == 0).astype(F32)
        tile = square[:, :HALF] + square[:, HALF:] + double + head * off
        lossb[b] = tile if j == 0 else lossb[b] + tile
        if j == nl - 1:
            each(nb, b, lambda k, q: put(LB, 0, lossb.at[b], lossb.at[b], s, q))

    def swap(j):
        got(AG, j, e.at[j, core, pl.ds(1, nc - 1)])
        put(EX, j, e.at[j, core], e.at[j, core], s, mate)

    def pull(j):
        mu = batch_mean(j)
        got(EX, j, e.at[j, 1 - core])
        c0 = (zall[j, :, :GROUP] - mu[:, :GROUP]).astype(BF16)
        c1 = (zall[j, :, GROUP:] - mu[:, GROUP:]).astype(BF16)
        e0, e1 = e[j, 0].reshape(GROUP, WIDE), e[j, 1].reshape(GROUP, WIDE)
        cross = jnp.concatenate([e0[:, GROUP:], e1[:, GROUP:]], axis=1)
        p0 = dot(c0, e0[:, :GROUP], ((1,), (0,))) + dot(c1, cross, ((1,), (1,)))
        p1 = dot(c0, cross, ((1,), (0,))) + dot(c1, e1[:, :GROUP], ((1,), (0,)))
        p = jnp.concatenate([p0, p1], axis=1) + 2.0 * (mu - pp[slot(j), 2:3, :])
        pall[j] = p.astype(BF16)

    def slopes(j):
        at = slot(j)
        scale = pp[at, 0:1, :]
        half = zall[j] * scale + pp[at, 1:2, :]
        t = jnp.tanh(half)
        slope[j] = (1.0 + t) * (1.0 + half * (1.0 - t)) * scale

    def backward():
        for g in range(BLOCK // GROUP):
            part = slice(g * GROUP, (g + 1) * GROUP)

            def layer(i, up):
                l = nl - 1 - i
                w = wall[slot(l)].reshape(BLOCK, GROUP)[part]
                grad = (up * slope[l, :, part] + pall[l, :, part].astype(F32)).astype(BF16)
                return dot(grad, w, ((1,), (1,))).astype(BF16).astype(F32)
            up = loop(nl, layer, jnp.zeros((rows, GROUP), F32))
            gout[:, :, part] = up.astype(BF16).reshape(nl, own_rows, GROUP)
        each(nl, s, lambda k, q: put(GO, block, gout.at[q], outv.at[block], q, b))
        outv[block] = gout[s]

    def loss_plane():
        got(LB, 0, lossb.at[pl.ds(1, nb - 1)])
        lossz[block] = jnp.sum(lossb[...], axis=0)
        each(nl, s, lambda k, q: put(LZ, block, lossz.at[block], lossz.at[block], q, b))

    def early_sends():
        sent(WC, wall.at[pl.ds(1, nl - 1), pl.ds(1, nc - 1), core])
        sent(WM, wall.at[pl.ds(1, nl - 1), :, core])
        sent(ZC, zc.at[:, core])
        sent(MM, mub.at[:, chip, core])
        sent(MC, mub.at[:, pl.ds(1, nc - 1)])
        sent(RS, srs.at[:, pl.ds(1, nc - 1)])
        sent(AG, e.at[:, core, pl.ds(1, nc - 1)])
        sent(EX, e.at[:, core])
        sent(LB, lossb.at[pl.ds(1, nb - 1)])

    @pl.when(s < nj)
    def _():
        gather_weights()
        last = nl - 1
        for t in range(nl + 4):
            for stage, delay in ((forward, 0), (gram, 1), (reduce, 3), (swap, 4), (pull, 5)):
                l = t - delay
                if 0 <= l < nl and not (stage is swap and l == last) and not (stage is pull and l >= last):
                    stage(l)
        for l in range(nl):
            slopes(l)
        swap(last)
        loss_plane()
        pull(last)
        backward()
        early_sends()
        sent(GO, gout.at[pl.ds(1, nl - 1)])
        sent(LZ, lossw.at[pl.ds(1, nl - 1)])

    def sent_layer(j):
        sent(WZ, w_ref.at[j, chip, core], j)
        sent(PP, ppo.at[j], j)
    planes(sent_layer)

    def arrived(j):
        got(LZ, j, lossz.at[j])
        got(GO, j, outv.at[j])
    planes(arrived)
    loss_ref[0, 0] = jnp.sum(jnp.sum(lossz[...], axis=0)) * (1.0 / (nl * nj * BLOCK))
    for j in range(nj):
        out_ref[:, j * BLOCK:(j + 1) * BLOCK] = outv[j]


def shards(nl, nb, images, weights, bn_mean, bn_var, bn_gain, bn_bias):
    rows, channels = images.shape[1:]
    nj = channels // BLOCK
    nc = nb // 2
    own_rows = rows // nl
    piece = GROUP // nc
    vmem, dma = pltpu.VMEM, pltpu.SemaphoreType.DMA
    halves = BLOCK // GROUP
    out, loss = pl.pallas_call(
        functools.partial(kernel, nl, nb, nj),
        out_shape=(jax.ShapeDtypeStruct((own_rows, channels), BF16),
                   jax.ShapeDtypeStruct((1, 1), F32)),
        in_specs=[pl.BlockSpec(memory_space=vmem)] * 6,
        out_specs=(pl.BlockSpec(memory_space=vmem), pl.BlockSpec(memory_space=pltpu.SMEM)),
        scratch_shapes=[
            vmem((nl, nc, 2, BLOCK // nb, GROUP), BF16),
            vmem((nl, 4, BLOCK), F32),
            vmem((nj, 4, BLOCK), F32),
            vmem((rows, BLOCK), BF16),
            vmem((nl, rows, BLOCK), F32),
            vmem((nl, rows, BLOCK), F32),
            vmem((nl, 2, halves, rows, GROUP), BF16),
            vmem((nl, nc, piece, WIDE), F32),
            vmem((nl, nc, piece, WIDE), BF16),
            vmem((nl, nc, piece, WIDE), BF16),
            vmem((nl, 2, nc, piece, WIDE), BF16),
            vmem((nl, rows, BLOCK), BF16),
            vmem((nl, own_rows, BLOCK), BF16),
            vmem((nj, own_rows, BLOCK), BF16),
            vmem((nl, nc, 2, 1, BLOCK), F32),
            vmem((1, BLOCK), F32),
            vmem((nb, 8, 128), F32),
            vmem((nj, 8, 128), F32),
            vmem((nl, 8, 128), F32),
            dma((13, nj)),
            dma((13, nl)),
        ],
        compiler_params=pltpu.CompilerParams(
            collective_id=0, has_side_effects=True, vmem_limit_bytes=60 * 1024 * 1024),
    )(images[0], weights.reshape(nj, nc, 2, BLOCK // nb, GROUP), bn_mean, bn_var, bn_gain, bn_bias)
    return (out[None], loss.reshape(()))


def solution(mesh):
    placed = (
        P("batch", None, None),
        P("section", None, None, None),
        P("section", None),
        P("section", None),
        P("section", None),
        P("section", None),
    )
    return jax.shard_map(
        functools.partial(shards, mesh.shape["section"], mesh.shape["batch"]),
        mesh=mesh,
        in_specs=placed,
        out_specs=(P("batch", "section", None), P()),
        check_vma=False,
    )
```

```python
import functools

import jax
import jax.numpy as jnp
from jax import lax
from jax.experimental import pallas as pl
from jax.experimental.pallas import tpu as pltpu
from jax.sharding import PartitionSpec as P

BLOCK = 512
GROUP = 256
HALF = 128
WIDE = GROUP + HALF
EPS = 1e-05
MESH = pl.DeviceIdType.MESH
F32 = jnp.float32
BF16 = jnp.bfloat16


def dot(a, b, dims):
    return lax.dot_general(a, b, (dims, ((), ())), preferred_element_type=F32)


def kernel(nl, nb, nj, x_ref, w_ref, mean_ref, var_ref, gain_ref, bias_ref, out_ref, loss_ref,
           wall, pp, ppo, xbuf, zall, slope, zc, sacc, srs, rs, e, pall, gout, outv, mub, mu_all, lossb, lossz, lossw,
           send, recv):
    s = lax.axis_index("section")
    b = lax.axis_index("batch")
    chip, core = b // 2, b % 2
    nc = nb // 2
    mate = chip * 2 + (1 - core)
    rows = x_ref.shape[0]
    own_rows = rows // nl
    piece = GROUP // nc
    row_total = rows * nb

    def copy(src, dst, ssem, rsem, sec, bat):
        return pltpu.make_async_remote_copy(
            src_ref=src, dst_ref=dst, send_sem=ssem, recv_sem=rsem,
            device_id=(sec, bat), device_id_type=MESH)

    def each(count, me, body):
        if count <= 8:
            for k in range(1, count):
                body(k, lax.rem(me + k, count))
        else:
            def step(k, carry):
                body(k, lax.rem(me + k, count))
                return carry
            lax.fori_loop(1, count, step, 0)

    def loop(count, body, carry):
        if count > 8:
            return lax.fori_loop(0, count, body, carry)
        for i in range(count):
            carry = body(i, carry)
        return carry

    def slot(l):
        return lax.rem(l - s + nl, nl)

    WZ, PP, WC, WM, ZC, MM, MC, RS, AG, EX, GO, LB, LZ = range(13)
    block = jnp.minimum(s, nj - 1)

    def got(kind, j, ref):
        copy(ref, ref, send.at[kind, 0], recv.at[kind, j], s, mate).wait_recv()

    def sent(kind, ref, j=0):
        copy(ref, ref, send.at[kind, j], recv.at[kind, 0], s, mate).wait_send()

    def put(kind, j, src, dst, sec, bat, out=0):
        copy(src, dst, send.at[kind, out], recv.at[kind, j], sec, bat).start()

    def planes(body):
        for j in range(nj):
            pl.when(j != s)(functools.partial(body, j))

    barrier = pltpu.get_barrier_semaphore()
    each(nb, b, lambda k, q: pl.semaphore_signal(barrier, inc=1, device_id=(s, q), device_id_type=MESH))
    each(nl, s, lambda k, q: pl.semaphore_signal(barrier, inc=1, device_id=(q, b), device_id_type=MESH))
    scale_own = gain_ref[...] * lax.rsqrt(var_ref[...] + EPS)
    shift_own = bias_ref[...] - mean_ref[...] * scale_own
    for j in range(nj):
        cols = slice(j * BLOCK, (j + 1) * BLOCK)
        ppo[j, 0:1, :] = 0.5 * scale_own[:, cols]
        ppo[j, 1:2, :] = 0.5 * shift_own[:, cols]
        ppo[j, 2:3, :] = mean_ref[:, cols]
        ppo[j, 3:4, :] = var_ref[:, cols]
    pp[0] = ppo[block]
    wall[0] = w_ref[block]
    pl.semaphore_wait(barrier, nb - 1 + nl - 1)

    def send_layer(j):
        at = lax.rem(s - j + nl, nl)
        put(WZ, s, w_ref.at[j, chip, core], wall.at[at, chip, core], j, b, j)
        put(PP, s, ppo.at[j], pp.at[at], j, b, j)
    planes(send_layer)

    def others(stage):
        return lambda l: pl.when(l != s)(functools.partial(stage, l))

    def spread_chips(l):
        mine = wall.at[slot(l), chip, core]
        got(WZ, l, mine)
        each(nc, chip, lambda k, q: put(WC, l, mine, mine, s, q * 2 + core))

    def spread_mate(l):
        got(WC, l, wall.at[slot(l), pl.ds(1, nc - 1), core])
        mine = wall.at[slot(l), :, core]
        put(WM, l, mine, mine, s, mate)

    def weights_here(l):
        got(WM, l, wall.at[slot(l), :, 1 - core])
        got(PP, l, pp.at[slot(l)])

    def forward(j):
        at = slot(j)
        others(weights_here)(j)
        w = wall[at].reshape(BLOCK, GROUP)
        for g in range(BLOCK // GROUP):
            part = slice(g * GROUP, (g + 1) * GROUP)
            z = dot(xbuf[:, part], w[part], ((1,), (0,)))
            zall[j, :, part] = z
            half = z * pp[at, 0:1, part] + pp[at, 1:2, part]
            xbuf[:, part] = (half + half * jnp.tanh(half)).astype(BF16)
        z = zall[j]
        mu = jnp.sum(z, axis=0, keepdims=True) * (1.0 / rows)
        mub[j, chip, core] = mu
        put(MM, j, mub.at[j, chip, core], mub.at[j, chip, core], s, mate)
        centered = (z - mu).astype(BF16)
        for h in range(BLOCK // GROUP):
            zc[j, core, h] = centered[:, h * GROUP:(h + 1) * GROUP]
        put(ZC, j, zc.at[j, core], zc.at[j, core], s, mate)

    def gram(j):
        got(MM, j, mub.at[j, chip, 1 - core])
        each(nc, chip, lambda k, q: put(MC, j, mub.at[j, chip], mub.at[j, chip], s, q * 2 + core))
        got(ZC, j, zc.at[j, 1 - core])
        cross = pl.ds(pl.multiple_of(core * HALF, HALF), HALF)
        square = dot(zc[j, 0, core], zc[j, 0, core], ((0,), (0,))) + dot(
            zc[j, 1, core], zc[j, 1, core], ((0,), (0,)))
        other = dot(zc[j, 0, 0], zc[j, 0, 1, :, cross], ((0,), (0,))) + dot(
            zc[j, 1, 0], zc[j, 1, 1, :, cross], ((0,), (0,)))
        total = jnp.concatenate([square, other], axis=1).reshape(nc, piece, WIDE)
        sacc[j] = total
        srs[j] = total.astype(BF16)
        each(nc, chip, lambda k, q: put(RS, j, srs.at[j, q], rs.at[j, nc - k], s, q * 2 + core))

    def batch_mean(j):
        return jnp.sum(mub[j], axis=(0, 1)) * (1.0 / nb)

    def reduce(j):
        at = slot(j)
        got(MC, j, mub.at[j, pl.ds(1, nc - 1)])
        mu = batch_mean(j)
        mine = pl.ds(pl.multiple_of(core * GROUP, GROUP), GROUP)
        cross = pl.ds(pl.multiple_of(GROUP + core * HALF, HALF), HALF)
        mu_all[...] = mu
        mu_mine, mu_cross, mu_low = mu_all[:, mine], mu_all[:, cross], mu[:, :GROUP]
        eye = (lax.broadcasted_iota(jnp.int32, (piece, GROUP), 0) + chip * piece
               == lax.broadcasted_iota(jnp.int32, (piece, GROUP), 1)).astype(F32)

        def between(i, acc):
            low = mub[j, i // 2, i % 2, :, :GROUP] - mu_low
            d_mine = mub[j, i // 2, i % 2, :, mine] - mu_mine
            d_cross = mub[j, i // 2, i % 2, :, cross] - mu_cross
            column = jnp.sum(eye * d_mine, axis=1, keepdims=True)
            column_low = jnp.sum(eye * low, axis=1, keepdims=True)
            return (acc[0] + column * d_mine, acc[1] + column_low * d_cross)
        corr = jnp.concatenate(loop(
            nb, between, (jnp.zeros((piece, GROUP), F32), jnp.zeros((piece, HALF), F32))), axis=1)
        cov = sacc[j, chip] + corr * rows
        got(RS, j, rs.at[j, pl.ds(1, nc - 1)])
        cov = loop(nc - 1, lambda i, acc: acc + rs[j, i + 1].astype(F32), cov) * (1.0 / row_total)
        dev, dev_cross = cov[:, :GROUP] - eye * pp[at, 3:4, mine], cov[:, GROUP:]
        e[j, core, chip] = jnp.concatenate([dev, dev_cross], axis=1).astype(BF16)
        own = e.at[j, core, chip]
        each(nc, chip, lambda k, q: put(AG, j, own, own, s, q * 2 + core))
        square = jnp.sum((dev * dev).reshape(piece // 8, 8, GROUP), axis=0) * 0.25
        double = jnp.sum((dev_cross * dev_cross).reshape(piece // 8, 8, HALF), axis=0) * 0.5
        off = mu - pp[at, 2:3, :]
        off = off * off
        off = sum(off[:, i * HALF:(i + 1) * HALF] for i in range(BLOCK // HALF))
        head = (lax.broadcasted_iota(jnp.int32, (8, HALF), 0) + b == 0).astype(F32)
        tile = square[:, :HALF] + square[:, HALF:] + double + head * off
        lossb[b] = tile if j == 0 else lossb[b] + tile
        if j == nl - 1:
            each(nb, b, lambda k, q: put(LB, 0, lossb.at[b], lossb.at[b], s, q))

    def swap(j):
        got(AG, j, e.at[j, core, pl.ds(1, nc - 1)])
        put(EX, j, e.at[j, core], e.at[j, core], s, mate)

    def pull(j):
        mu = batch_mean(j)
        got(EX, j, e.at[j, 1 - core])
        c0 = (zall[j, :, :GROUP] - mu[:, :GROUP]).astype(BF16)
        c1 = (zall[j, :, GROUP:] - mu[:, GROUP:]).astype(BF16)
        e0, e1 = e[j, 0].reshape(GROUP, WIDE), e[j, 1].reshape(GROUP, WIDE)
        cross = jnp.concatenate([e0[:, GROUP:], e1[:, GROUP:]], axis=1)
        p0 = dot(c0, e0[:, :GROUP], ((1,), (0,))) + dot(c1, cross, ((1,), (1,)))
        p1 = dot(c0, cross, ((1,), (0,))) + dot(c1, e1[:, :GROUP], ((1,), (0,)))
        p = jnp.concatenate([p0, p1], axis=1) + 2.0 * (mu - pp[slot(j), 2:3, :])
        pall[j] = p.astype(BF16)

    def slopes(j):
        at = slot(j)
        scale = pp[at, 0:1, :]
        half = zall[j] * scale + pp[at, 1:2, :]
        t = jnp.tanh(half)
        slope[j] = (1.0 + t) * (1.0 + half * (1.0 - t)) * scale

    def backward():
        for g in range(BLOCK // GROUP):
            part = slice(g * GROUP, (g + 1) * GROUP)

            def layer(i, up):
                l = nl - 1 - i
                w = wall[slot(l)].reshape(BLOCK, GROUP)[part]
                grad = (up * slope[l, :, part] + pall[l, :, part].astype(F32)).astype(BF16)
                return dot(grad, w, ((1,), (1,))).astype(BF16).astype(F32)
            up = loop(nl, layer, jnp.zeros((rows, GROUP), F32))
            gout[g] = up.astype(BF16).reshape(nl, own_rows, GROUP)
            each(nl, s, lambda k, q: put(GO, g * nl + block, gout.at[g, q], outv.at[block, g], q, b))
        for g in range(BLOCK // GROUP):
            outv[block, g] = gout[g, s]

    def loss_plane():
        got(LB, 0, lossb.at[pl.ds(1, nb - 1)])
        lossz[block] = jnp.sum(lossb[...], axis=0)
        each(nl, s, lambda k, q: put(LZ, block, lossz.at[block], lossz.at[block], q, b))

    def early_sends():
        sent(WC, wall.at[pl.ds(1, nl - 1), pl.ds(1, nc - 1), core])
        sent(WM, wall.at[pl.ds(1, nl - 1), :, core])
        sent(ZC, zc.at[:, core])
        sent(MM, mub.at[:, chip, core])
        sent(MC, mub.at[:, pl.ds(1, nc - 1)])
        sent(RS, srs.at[:, pl.ds(1, nc - 1)])
        sent(AG, e.at[:, core, pl.ds(1, nc - 1)])
        sent(EX, e.at[:, core])
        sent(LB, lossb.at[pl.ds(1, nb - 1)])

    @pl.when(s < nj)
    def _():
        xbuf[...] = x_ref[:, pl.ds(pl.multiple_of(block * BLOCK, BLOCK), BLOCK)]
        for l in range(nl):
            others(spread_chips)(l)
        last = nl - 1
        for t in range(nl + 5):
            for stage, delay in ((others(spread_mate), 0), (forward, 1), (gram, 2), (reduce, 4), (swap, 5), (pull, 6)):
                l = t - delay
                if 0 <= l < nl and not (stage is swap and l == last) and not (stage is pull and l >= last):
                    stage(l)
        for l in range(nl):
            slopes(l)
        swap(last)
        loss_plane()
        pull(last)
        backward()
        early_sends()
        sent(GO, gout.at[:, pl.ds(1, nl - 1)])
        sent(LZ, lossw.at[pl.ds(1, nl - 1)])

    def sent_layer(j):
        sent(WZ, w_ref.at[j, chip, core], j)
        sent(PP, ppo.at[j], j)
    planes(sent_layer)

    def arrived(j):
        got(LZ, j, lossz.at[j])
        for g in range(BLOCK // GROUP):
            got(GO, g * nl + j, outv.at[j, g])
    planes(arrived)
    loss_ref[0, 0] = jnp.sum(jnp.sum(lossz[...], axis=0)) * (1.0 / (nl * nj * BLOCK))
    for j in range(nj):
        for g in range(BLOCK // GROUP):
            out_ref[:, j * BLOCK + g * GROUP:j * BLOCK + (g + 1) * GROUP] = outv[j, g]


def shards(nl, nb, images, weights, bn_mean, bn_var, bn_gain, bn_bias):
    rows, channels = images.shape[1:]
    nj = channels // BLOCK
    nc = nb // 2
    own_rows = rows // nl
    piece = GROUP // nc
    vmem, dma = pltpu.VMEM, pltpu.SemaphoreType.DMA
    halves = BLOCK // GROUP
    out, loss = pl.pallas_call(
        functools.partial(kernel, nl, nb, nj),
        out_shape=(jax.ShapeDtypeStruct((own_rows, channels), BF16),
                   jax.ShapeDtypeStruct((1, 1), F32)),
        in_specs=[pl.BlockSpec(memory_space=vmem)] * 6,
        out_specs=(pl.BlockSpec(memory_space=vmem), pl.BlockSpec(memory_space=pltpu.SMEM)),
        scratch_shapes=[
            vmem((nl, nc, 2, BLOCK // nb, GROUP), BF16),
            vmem((nl, 4, BLOCK), F32),
            vmem((nj, 4, BLOCK), F32),
            vmem((rows, BLOCK), BF16),
            vmem((nl, rows, BLOCK), F32),
            vmem((nl, rows, BLOCK), F32),
            vmem((nl, 2, halves, rows, GROUP), BF16),
            vmem((nl, nc, piece, WIDE), F32),
            vmem((nl, nc, piece, WIDE), BF16),
            vmem((nl, nc, piece, WIDE), BF16),
            vmem((nl, 2, nc, piece, WIDE), BF16),
            vmem((nl, rows, BLOCK), BF16),
            vmem((halves, nl, own_rows, GROUP), BF16),
            vmem((nj, halves, own_rows, GROUP), BF16),
            vmem((nl, nc, 2, 1, BLOCK), F32),
            vmem((1, BLOCK), F32),
            vmem((nb, 8, 128), F32),
            vmem((nj, 8, 128), F32),
            vmem((nl, 8, 128), F32),
            dma((13, nj)),
            dma((13, 2 * nl)),
        ],
        compiler_params=pltpu.CompilerParams(
            collective_id=0, has_side_effects=True, vmem_limit_bytes=60 * 1024 * 1024),
    )(images[0], weights.reshape(nj, nc, 2, BLOCK // nb, GROUP), bn_mean, bn_var, bn_gain, bn_bias)
    return (out[None], loss.reshape(()))


def solution(mesh):
    placed = (
        P("batch", None, None),
        P("section", None, None, None),
        P("section", None),
        P("section", None),
        P("section", None),
        P("section", None),
    )
    return jax.shard_map(
        functools.partial(shards, mesh.shape["section"], mesh.shape["batch"]),
        mesh=mesh,
        in_specs=placed,
        out_specs=(P("batch", "section", None), P()),
        check_vma=False,
    )
```

```python
import functools

import jax
import jax.numpy as jnp
from jax import lax
from jax.experimental import pallas as pl
from jax.experimental.pallas import tpu as pltpu
from jax.sharding import PartitionSpec as P

BLOCK = 512
GROUP = 256
HALF = 128
WIDE = GROUP + HALF
EPS = 1e-05
MESH = pl.DeviceIdType.MESH
F32 = jnp.float32
BF16 = jnp.bfloat16


def dot(a, b, dims):
    return lax.dot_general(a, b, (dims, ((), ())), preferred_element_type=F32)


def kernel(nl, nb, nj, x_ref, w_ref, mean_ref, var_ref, gain_ref, bias_ref, out_ref, loss_ref,
           wall, pp, ppo, xbuf, zall, slope, zc, sacc, srs, rs, e, pall, gout, outv, mub, mu_all, lossb, lossz, lossw,
           send, recv):
    s = lax.axis_index("section")
    b = lax.axis_index("batch")
    chip, core = b // 2, b % 2
    nc = nb // 2
    mate = chip * 2 + (1 - core)
    rows = x_ref.shape[0]
    own_rows = rows // nl
    piece = GROUP // nc
    row_total = rows * nb

    def copy(src, dst, ssem, rsem, sec, bat):
        return pltpu.make_async_remote_copy(
            src_ref=src, dst_ref=dst, send_sem=ssem, recv_sem=rsem,
            device_id=(sec, bat), device_id_type=MESH)

    def each(count, me, body):
        if count <= 8:
            for k in range(1, count):
                body(k, lax.rem(me + k, count))
        else:
            def step(k, carry):
                body(k, lax.rem(me + k, count))
                return carry
            lax.fori_loop(1, count, step, 0)

    def loop(count, body, carry):
        if count > 8:
            return lax.fori_loop(0, count, body, carry)
        for i in range(count):
            carry = body(i, carry)
        return carry

    def slot(l):
        return lax.rem(l - s + nl, nl)

    WZ, PP, WC, WM, ZC, MM, MC, RS, AG, EX, GO, LB, LZ = range(13)
    block = jnp.minimum(s, nj - 1)

    def got(kind, j, ref):
        copy(ref, ref, send.at[kind, 0], recv.at[kind, j], s, mate).wait_recv()

    def sent(kind, ref, j=0):
        copy(ref, ref, send.at[kind, j], recv.at[kind, 0], s, mate).wait_send()

    def put(kind, j, src, dst, sec, bat, out=0):
        copy(src, dst, send.at[kind, out], recv.at[kind, j], sec, bat).start()

    def planes(body):
        for j in range(nj):
            pl.when(j != s)(functools.partial(body, j))

    barrier = pltpu.get_barrier_semaphore()
    each(nb, b, lambda k, q: pl.semaphore_signal(barrier, inc=1, device_id=(s, q), device_id_type=MESH))
    each(nl, s, lambda k, q: pl.semaphore_signal(barrier, inc=1, device_id=(q, b), device_id_type=MESH))
    scale_own = gain_ref[...] * lax.rsqrt(var_ref[...] + EPS)
    shift_own = bias_ref[...] - mean_ref[...] * scale_own
    for j in range(nj):
        cols = slice(j * BLOCK, (j + 1) * BLOCK)
        ppo[j, 0:1, :] = 0.5 * scale_own[:, cols]
        ppo[j, 1:2, :] = 0.5 * shift_own[:, cols]
        ppo[j, 2:3, :] = mean_ref[:, cols]
        ppo[j, 3:4, :] = var_ref[:, cols]
    pp[0] = ppo[block]
    wall[0] = w_ref[block]
    pl.semaphore_wait(barrier, nb - 1 + nl - 1)

    def send_layer(j):
        at = lax.rem(s - j + nl, nl)
        put(WZ, s, w_ref.at[j, chip, core], wall.at[at, chip, core], j, b, j)
        put(PP, s, ppo.at[j], pp.at[at], j, b, j)
    planes(send_layer)

    def others(stage):
        return lambda l: pl.when(l != s)(functools.partial(stage, l))

    def spread_chips(l):
        mine = wall.at[slot(l), chip, core]
        got(WZ, l, mine)
        each(nc, chip, lambda k, q: put(WC, l, mine, mine, s, q * 2 + core))

    def spread_mate(l):
        got(WC, l, wall.at[slot(l), pl.ds(1, nc - 1), core])
        mine = wall.at[slot(l), :, core]
        put(WM, l, mine, mine, s, mate)

    def weights_here(l):
        got(WM, l, wall.at[slot(l), :, 1 - core])
        got(PP, l, pp.at[slot(l)])

    def forward(j):
        at = slot(j)
        others(weights_here)(j)
        w = wall[at].reshape(BLOCK, GROUP)
        for g in range(BLOCK // GROUP):
            part = slice(g * GROUP, (g + 1) * GROUP)
            z = dot(xbuf[:, part], w[part], ((1,), (0,)))
            zall[j, :, part] = z
            half = z * pp[at, 0:1, part] + pp[at, 1:2, part]
            xbuf[:, part] = (half + half * jnp.tanh(half)).astype(BF16)
        z = zall[j]
        mu = jnp.sum(z, axis=0, keepdims=True) * (1.0 / rows)
        mub[j, chip, core] = mu
        put(MM, j, mub.at[j, chip, core], mub.at[j, chip, core], s, mate)
        centered = (z - mu).astype(BF16)
        for h in range(BLOCK // GROUP):
            zc[j, core, h] = centered[:, h * GROUP:(h + 1) * GROUP]
        put(ZC, j, zc.at[j, core], zc.at[j, core], s, mate)

    def gram(j):
        got(MM, j, mub.at[j, chip, 1 - core])
        each(nc, chip, lambda k, q: put(MC, j, mub.at[j, chip], mub.at[j, chip], s, q * 2 + core))
        got(ZC, j, zc.at[j, 1 - core])
        cross = pl.ds(pl.multiple_of(core * HALF, HALF), HALF)
        square = dot(zc[j, 0, core], zc[j, 0, core], ((0,), (0,))) + dot(
            zc[j, 1, core], zc[j, 1, core], ((0,), (0,)))
        other = dot(zc[j, 0, 0], zc[j, 0, 1, :, cross], ((0,), (0,))) + dot(
            zc[j, 1, 0], zc[j, 1, 1, :, cross], ((0,), (0,)))
        total = jnp.concatenate([square, other], axis=1).reshape(nc, piece, WIDE)
        sacc[j] = total
        srs[j] = total.astype(BF16)
        each(nc, chip, lambda k, q: put(RS, j, srs.at[j, q], rs.at[j, nc - k], s, q * 2 + core))

    def batch_mean(j):
        return jnp.sum(mub[j], axis=(0, 1)) * (1.0 / nb)

    def reduce(j):
        at = slot(j)
        got(MC, j, mub.at[j, pl.ds(1, nc - 1)])
        mu = batch_mean(j)
        mine = pl.ds(pl.multiple_of(core * GROUP, GROUP), GROUP)
        cross = pl.ds(pl.multiple_of(GROUP + core * HALF, HALF), HALF)
        mu_all[...] = mu
        mu_mine, mu_cross, mu_low = mu_all[:, mine], mu_all[:, cross], mu[:, :GROUP]
        eye = (lax.broadcasted_iota(jnp.int32, (piece, GROUP), 0) + chip * piece
               == lax.broadcasted_iota(jnp.int32, (piece, GROUP), 1)).astype(F32)

        def between(i, acc):
            low = mub[j, i // 2, i % 2, :, :GROUP] - mu_low
            d_mine = mub[j, i // 2, i % 2, :, mine] - mu_mine
            d_cross = mub[j, i // 2, i % 2, :, cross] - mu_cross
            column = jnp.sum(eye * d_mine, axis=1, keepdims=True)
            column_low = jnp.sum(eye * low, axis=1, keepdims=True)
            return (acc[0] + column * d_mine, acc[1] + column_low * d_cross)
        corr = jnp.concatenate(loop(
            nb, between, (jnp.zeros((piece, GROUP), F32), jnp.zeros((piece, HALF), F32))), axis=1)
        cov = sacc[j, chip] + corr * rows
        got(RS, j, rs.at[j, pl.ds(1, nc - 1)])
        cov = loop(nc - 1, lambda i, acc: acc + rs[j, i + 1].astype(F32), cov) * (1.0 / row_total)
        dev, dev_cross = cov[:, :GROUP] - eye * pp[at, 3:4, mine], cov[:, GROUP:]
        e[j, core, chip] = jnp.concatenate([dev, dev_cross], axis=1).astype(BF16)
        own = e.at[j, core, chip]
        each(nc, chip, lambda k, q: put(AG, j, own, own, s, q * 2 + core))
        square = jnp.sum((dev * dev).reshape(piece // 8, 8, GROUP), axis=0) * 0.25
        double = jnp.sum((dev_cross * dev_cross).reshape(piece // 8, 8, HALF), axis=0) * 0.5
        off = mu - pp[at, 2:3, :]
        off = off * off
        off = sum(off[:, i * HALF:(i + 1) * HALF] for i in range(BLOCK // HALF))
        head = (lax.broadcasted_iota(jnp.int32, (8, HALF), 0) + b == 0).astype(F32)
        tile = square[:, :HALF] + square[:, HALF:] + double + head * off
        lossb[b] = tile if j == 0 else lossb[b] + tile
        if j == nl - 1:
            each(nb, b, lambda k, q: put(LB, 0, lossb.at[b], lossb.at[b], s, q))

    def swap(j):
        got(AG, j, e.at[j, core, pl.ds(1, nc - 1)])
        put(EX, j, e.at[j, core], e.at[j, core], s, mate)

    def pull(j):
        mu = batch_mean(j)
        got(EX, j, e.at[j, 1 - core])
        c0 = (zall[j, :, :GROUP] - mu[:, :GROUP]).astype(BF16)
        c1 = (zall[j, :, GROUP:] - mu[:, GROUP:]).astype(BF16)
        e0, e1 = e[j, 0].reshape(GROUP, WIDE), e[j, 1].reshape(GROUP, WIDE)
        cross = jnp.concatenate([e0[:, GROUP:], e1[:, GROUP:]], axis=1)
        p0 = dot(c0, e0[:, :GROUP], ((1,), (0,))) + dot(c1, cross, ((1,), (1,)))
        p1 = dot(c0, cross, ((1,), (0,))) + dot(c1, e1[:, :GROUP], ((1,), (0,)))
        p = jnp.concatenate([p0, p1], axis=1) + 2.0 * (mu - pp[slot(j), 2:3, :])
        pall[j] = p.astype(BF16)

    def slopes(j):
        at = slot(j)
        scale = pp[at, 0:1, :]
        half = zall[j] * scale + pp[at, 1:2, :]
        t = jnp.tanh(half)
        slope[j] = (1.0 + t) * (1.0 + half * (1.0 - t)) * scale

    def backward():
        for g in range(BLOCK // GROUP):
            part = slice(g * GROUP, (g + 1) * GROUP)

            def layer(i, up):
                l = nl - 1 - i
                w = wall[slot(l)].reshape(BLOCK, GROUP)[part]
                grad = (up * slope[l, :, part] + pall[l, :, part].astype(F32)).astype(BF16)
                return dot(grad, w, ((1,), (1,))).astype(BF16).astype(F32)
            up = loop(nl, layer, jnp.zeros((rows, GROUP), F32))
            gout[g] = up.astype(BF16).reshape(nl, own_rows, GROUP)
            each(nl, s, lambda k, q: put(GO, g * nl + block, gout.at[g, q], outv.at[block, g], q, b))
        for g in range(BLOCK // GROUP):
            outv[block, g] = gout[g, s]

    def loss_plane():
        got(LB, 0, lossb.at[pl.ds(1, nb - 1)])
        lossz[block] = jnp.sum(lossb[...], axis=0)
        each(nl, s, lambda k, q: put(LZ, block, lossz.at[block], lossz.at[block], q, b))

    def early_sends():
        sent(WC, wall.at[pl.ds(1, nl - 1), pl.ds(1, nc - 1), core])
        sent(WM, wall.at[pl.ds(1, nl - 1), :, core])
        sent(ZC, zc.at[:, core])
        sent(MM, mub.at[:, chip, core])
        sent(MC, mub.at[:, pl.ds(1, nc - 1)])
        sent(RS, srs.at[:, pl.ds(1, nc - 1)])
        sent(AG, e.at[:, core, pl.ds(1, nc - 1)])
        sent(EX, e.at[:, core])
        sent(LB, lossb.at[pl.ds(1, nb - 1)])

    @pl.when(s < nj)
    def _():
        xbuf[...] = x_ref[:, pl.ds(pl.multiple_of(block * BLOCK, BLOCK), BLOCK)]
        for l in range(nl):
            others(spread_chips)(l)
        last = nl - 1
        for t in range(nl + 7):
            for stage, delay in ((others(spread_mate), 0), (forward, 1), (gram, 2), (reduce, 4), (slopes, 5), (swap, 7), (pull, 8)):
                l = t - delay
                if 0 <= l < nl and not (stage is swap and l == last) and not (stage is pull and l >= last):
                    stage(l)
        swap(last)
        loss_plane()
        pull(last)
        backward()
        early_sends()
        sent(GO, gout.at[:, pl.ds(1, nl - 1)])
        sent(LZ, lossw.at[pl.ds(1, nl - 1)])

    def sent_layer(j):
        sent(WZ, w_ref.at[j, chip, core], j)
        sent(PP, ppo.at[j], j)
    planes(sent_layer)

    def arrived(j):
        got(LZ, j, lossz.at[j])
        for g in range(BLOCK // GROUP):
            got(GO, g * nl + j, outv.at[j, g])
    planes(arrived)
    loss_ref[0, 0] = jnp.sum(jnp.sum(lossz[...], axis=0)) * (1.0 / (nl * nj * BLOCK))
    for j in range(nj):
        for g in range(BLOCK // GROUP):
            out_ref[:, j * BLOCK + g * GROUP:j * BLOCK + (g + 1) * GROUP] = outv[j, g]


def shards(nl, nb, images, weights, bn_mean, bn_var, bn_gain, bn_bias):
    rows, channels = images.shape[1:]
    nj = channels // BLOCK
    nc = nb // 2
    own_rows = rows // nl
    piece = GROUP // nc
    vmem, dma = pltpu.VMEM, pltpu.SemaphoreType.DMA
    halves = BLOCK // GROUP
    out, loss = pl.pallas_call(
        functools.partial(kernel, nl, nb, nj),
        out_shape=(jax.ShapeDtypeStruct((own_rows, channels), BF16),
                   jax.ShapeDtypeStruct((1, 1), F32)),
        in_specs=[pl.BlockSpec(memory_space=vmem)] * 6,
        out_specs=(pl.BlockSpec(memory_space=vmem), pl.BlockSpec(memory_space=pltpu.SMEM)),
        scratch_shapes=[
            vmem((nl, nc, 2, BLOCK // nb, GROUP), BF16),
            vmem((nl, 4, BLOCK), F32),
            vmem((nj, 4, BLOCK), F32),
            vmem((rows, BLOCK), BF16),
            vmem((nl, rows, BLOCK), F32),
            vmem((nl, rows, BLOCK), F32),
            vmem((nl, 2, halves, rows, GROUP), BF16),
            vmem((nl, nc, piece, WIDE), F32),
            vmem((nl, nc, piece, WIDE), BF16),
            vmem((nl, nc, piece, WIDE), BF16),
            vmem((nl, 2, nc, piece, WIDE), BF16),
            vmem((nl, rows, BLOCK), BF16),
            vmem((halves, nl, own_rows, GROUP), BF16),
            vmem((nj, halves, own_rows, GROUP), BF16),
            vmem((nl, nc, 2, 1, BLOCK), F32),
            vmem((1, BLOCK), F32),
            vmem((nb, 8, 128), F32),
            vmem((nj, 8, 128), F32),
            vmem((nl, 8, 128), F32),
            dma((13, nj)),
            dma((13, 2 * nl)),
        ],
        compiler_params=pltpu.CompilerParams(
            collective_id=0, has_side_effects=True, vmem_limit_bytes=60 * 1024 * 1024),
    )(images[0], weights.reshape(nj, nc, 2, BLOCK // nb, GROUP), bn_mean, bn_var, bn_gain, bn_bias)
    return (out[None], loss.reshape(()))


def solution(mesh):
    placed = (
        P("batch", None, None),
        P("section", None, None, None),
        P("section", None),
        P("section", None),
        P("section", None),
        P("section", None),
    )
    return jax.shard_map(
        functools.partial(shards, mesh.shape["section"], mesh.shape["batch"]),
        mesh=mesh,
        in_specs=placed,
        out_specs=(P("batch", "section", None), P()),
        check_vma=False,
    )
```

```python
import functools

import jax
import jax.numpy as jnp
from jax import lax
from jax.experimental import pallas as pl
from jax.experimental.pallas import tpu as pltpu
from jax.sharding import PartitionSpec as P

BLOCK = 512
GROUP = 256
HALF = 128
WIDE = GROUP + HALF
EPS = 1e-05
MESH = pl.DeviceIdType.MESH
F32 = jnp.float32
BF16 = jnp.bfloat16


def dot(a, b, dims):
    return lax.dot_general(a, b, (dims, ((), ())), preferred_element_type=F32)


def kernel(nl, nb, nj, x_ref, w_ref, mean_ref, var_ref, gain_ref, bias_ref, out_ref, loss_ref,
           wall, pp, ppo, xbuf, zall, slope, zc, sacc, srs, rs, e, pall, gout, outv, mub, mu_all, lossb, lossz, lossw,
           send, recv):
    s = lax.axis_index("section")
    b = lax.axis_index("batch")
    chip, core = b // 2, b % 2
    nc = nb // 2
    mate = chip * 2 + (1 - core)
    rows = x_ref.shape[0]
    own_rows = rows // nl
    piece = GROUP // nc
    row_total = rows * nb

    def copy(src, dst, ssem, rsem, sec, bat):
        return pltpu.make_async_remote_copy(
            src_ref=src, dst_ref=dst, send_sem=ssem, recv_sem=rsem,
            device_id=(sec, bat), device_id_type=MESH)

    def each(count, me, body):
        if count <= 8:
            for k in range(1, count):
                body(k, lax.rem(me + k, count))
        else:
            def step(k, carry):
                body(k, lax.rem(me + k, count))
                return carry
            lax.fori_loop(1, count, step, 0)

    def loop(count, body, carry):
        if count > 8:
            return lax.fori_loop(0, count, body, carry)
        for i in range(count):
            carry = body(i, carry)
        return carry

    def slot(l):
        return lax.rem(l - s + nl, nl)

    WZ, PP, WC, WM, ZC, MM, MC, RS, AG, EX, GO, LB, LZ = range(13)
    block = jnp.minimum(s, nj - 1)

    def got(kind, j, ref):
        copy(ref, ref, send.at[kind, 0], recv.at[kind, j], s, mate).wait_recv()

    def sent(kind, ref, j=0):
        copy(ref, ref, send.at[kind, j], recv.at[kind, 0], s, mate).wait_send()

    def put(kind, j, src, dst, sec, bat, out=0):
        copy(src, dst, send.at[kind, out], recv.at[kind, j], sec, bat).start()

    def planes(body):
        for j in range(nj):
            pl.when(j != s)(functools.partial(body, j))

    barrier = pltpu.get_barrier_semaphore()
    each(nb, b, lambda k, q: pl.semaphore_signal(barrier, inc=1, device_id=(s, q), device_id_type=MESH))
    each(nl, s, lambda k, q: pl.semaphore_signal(barrier, inc=1, device_id=(q, b), device_id_type=MESH))
    scale_own = gain_ref[...] * lax.rsqrt(var_ref[...] + EPS)
    shift_own = bias_ref[...] - mean_ref[...] * scale_own
    for j in range(nj):
        cols = slice(j * BLOCK, (j + 1) * BLOCK)
        ppo[j, 0:1, :] = 0.5 * scale_own[:, cols]
        ppo[j, 1:2, :] = 0.5 * shift_own[:, cols]
        ppo[j, 2:3, :] = mean_ref[:, cols]
        ppo[j, 3:4, :] = var_ref[:, cols]
    pp[0] = ppo[block]
    wall[0] = w_ref[block]
    pl.semaphore_wait(barrier, nb - 1 + nl - 1)

    def send_layer(j):
        at = lax.rem(s - j + nl, nl)
        put(WZ, s, w_ref.at[j, chip, core], wall.at[at, chip, core], j, b, j)
        put(PP, s, ppo.at[j], pp.at[at], j, b, j)
    planes(send_layer)

    def others(stage):
        return lambda l: pl.when(l != s)(functools.partial(stage, l))

    def spread_chips(l):
        mine = wall.at[slot(l), chip, core]
        got(WZ, l, mine)
        each(nc, chip, lambda k, q: put(WC, l, mine, mine, s, q * 2 + core))

    def spread_mate(l):
        got(WC, l, wall.at[slot(l), pl.ds(1, nc - 1), core])
        mine = wall.at[slot(l), :, core]
        put(WM, l, mine, mine, s, mate)

    def weights_here(l):
        got(WM, l, wall.at[slot(l), :, 1 - core])
        got(PP, l, pp.at[slot(l)])

    def forward(j):
        at = slot(j)
        others(weights_here)(j)
        w = wall[at].reshape(BLOCK, GROUP)
        for g in range(BLOCK // GROUP):
            part = slice(g * GROUP, (g + 1) * GROUP)
            z = dot(xbuf[:, part], w[part], ((1,), (0,)))
            zall[j, :, part] = z
            half = z * pp[at, 0:1, part] + pp[at, 1:2, part]
            xbuf[:, part] = (half + half * jnp.tanh(half)).astype(BF16)
        z = zall[j]
        mu = jnp.sum(z, axis=0, keepdims=True) * (1.0 / rows)
        mub[j, chip, core] = mu
        put(MM, j, mub.at[j, chip, core], mub.at[j, chip, core], s, mate)
        centered = (z - mu).astype(BF16)
        for h in range(BLOCK // GROUP):
            zc[j, core, h] = centered[:, h * GROUP:(h + 1) * GROUP]
        put(ZC, j, zc.at[j, core], zc.at[j, core], s, mate)

    def gram(j):
        got(MM, j, mub.at[j, chip, 1 - core])
        each(nc, chip, lambda k, q: put(MC, j, mub.at[j, chip], mub.at[j, chip], s, q * 2 + core))
        got(ZC, j, zc.at[j, 1 - core])
        cross = pl.ds(pl.multiple_of(core * HALF, HALF), HALF)
        square = dot(zc[j, 0, core], zc[j, 0, core], ((0,), (0,))) + dot(
            zc[j, 1, core], zc[j, 1, core], ((0,), (0,)))
        other = dot(zc[j, 0, 0], zc[j, 0, 1, :, cross], ((0,), (0,))) + dot(
            zc[j, 1, 0], zc[j, 1, 1, :, cross], ((0,), (0,)))
        total = jnp.concatenate([square, other], axis=1).reshape(nc, piece, WIDE)
        sacc[j] = total
        srs[j] = total.astype(BF16)
        each(nc, chip, lambda k, q: put(RS, j, srs.at[j, q], rs.at[j, nc - k], s, q * 2 + core))

    def batch_mean(j):
        return jnp.sum(mub[j], axis=(0, 1)) * (1.0 / nb)

    def reduce(j):
        at = slot(j)
        got(MC, j, mub.at[j, pl.ds(1, nc - 1)])
        mu = batch_mean(j)
        mine = pl.ds(pl.multiple_of(core * GROUP, GROUP), GROUP)
        cross = pl.ds(pl.multiple_of(GROUP + core * HALF, HALF), HALF)
        mu_all[...] = mu
        mu_mine, mu_cross, mu_low = mu_all[:, mine], mu_all[:, cross], mu[:, :GROUP]
        eye = (lax.broadcasted_iota(jnp.int32, (piece, GROUP), 0) + chip * piece
               == lax.broadcasted_iota(jnp.int32, (piece, GROUP), 1)).astype(F32)

        def between(i, acc):
            low = mub[j, i // 2, i % 2, :, :GROUP] - mu_low
            d_mine = mub[j, i // 2, i % 2, :, mine] - mu_mine
            d_cross = mub[j, i // 2, i % 2, :, cross] - mu_cross
            column = jnp.sum(eye * d_mine, axis=1, keepdims=True)
            column_low = jnp.sum(eye * low, axis=1, keepdims=True)
            return (acc[0] + column * d_mine, acc[1] + column_low * d_cross)
        corr = jnp.concatenate(loop(
            nb, between, (jnp.zeros((piece, GROUP), F32), jnp.zeros((piece, HALF), F32))), axis=1)
        cov = sacc[j, chip] + corr * rows
        got(RS, j, rs.at[j, pl.ds(1, nc - 1)])
        cov = loop(nc - 1, lambda i, acc: acc + rs[j, i + 1].astype(F32), cov) * (1.0 / row_total)
        dev, dev_cross = cov[:, :GROUP] - eye * pp[at, 3:4, mine], cov[:, GROUP:]
        e[j, core, chip] = jnp.concatenate([dev, dev_cross], axis=1).astype(BF16)
        own = e.at[j, core, chip]
        each(nc, chip, lambda k, q: put(AG, j, own, own, s, q * 2 + core))
        square = jnp.sum((dev * dev).reshape(piece // 8, 8, GROUP), axis=0) * 0.25
        double = jnp.sum((dev_cross * dev_cross).reshape(piece // 8, 8, HALF), axis=0) * 0.5
        off = mu - pp[at, 2:3, :]
        off = off * off
        off = sum(off[:, i * HALF:(i + 1) * HALF] for i in range(BLOCK // HALF))
        head = (lax.broadcasted_iota(jnp.int32, (8, HALF), 0) + b == 0).astype(F32)
        tile = square[:, :HALF] + square[:, HALF:] + double + head * off
        lossb[b] = tile if j == 0 else lossb[b] + tile
        if j == nl - 1:
            each(nb, b, lambda k, q: put(LB, 0, lossb.at[b], lossb.at[b], s, q))

    def swap(j):
        got(AG, j, e.at[j, core, pl.ds(1, nc - 1)])
        put(EX, j, e.at[j, core], e.at[j, core], s, mate)

    def pull(j):
        mu = batch_mean(j)
        got(EX, j, e.at[j, 1 - core])
        c0 = (zall[j, :, :GROUP] - mu[:, :GROUP]).astype(BF16)
        c1 = (zall[j, :, GROUP:] - mu[:, GROUP:]).astype(BF16)
        e0, e1 = e[j, 0].reshape(GROUP, WIDE), e[j, 1].reshape(GROUP, WIDE)
        cross = jnp.concatenate([e0[:, GROUP:], e1[:, GROUP:]], axis=1)
        p0 = dot(c0, e0[:, :GROUP], ((1,), (0,))) + dot(c1, cross, ((1,), (1,)))
        p1 = dot(c0, cross, ((1,), (0,))) + dot(c1, e1[:, :GROUP], ((1,), (0,)))
        p = jnp.concatenate([p0, p1], axis=1) + 2.0 * (mu - pp[slot(j), 2:3, :])
        pall[j] = p.astype(BF16)

    def slopes(j):
        at = slot(j)
        scale = pp[at, 0:1, :]
        half = zall[j] * scale + pp[at, 1:2, :]
        t = jnp.tanh(half)
        slope[j] = (1.0 + t) * (1.0 + half * (1.0 - t)) * scale

    def backward():
        for g in range(BLOCK // GROUP):
            part = slice(g * GROUP, (g + 1) * GROUP)

            def layer(i, up):
                l = nl - 1 - i
                w = wall[slot(l)].reshape(BLOCK, GROUP)[part]
                grad = (up * slope[l, :, part] + pall[l, :, part].astype(F32)).astype(BF16)
                return dot(grad, w, ((1,), (1,))).astype(BF16).astype(F32)
            up = loop(nl, layer, jnp.zeros((rows, GROUP), F32))
            gout[g] = up.astype(BF16).reshape(nl, own_rows, GROUP)
            each(nl, s, lambda k, q: put(GO, g * nl + block, gout.at[g, q], outv.at[block, g], q, b))
        for g in range(BLOCK // GROUP):
            outv[block, g] = gout[g, s]

    def loss_plane():
        got(LB, 0, lossb.at[pl.ds(1, nb - 1)])
        lossz[block] = jnp.sum(lossb[...], axis=0)
        each(nl, s, lambda k, q: put(LZ, block, lossz.at[block], lossz.at[block], q, b))

    def early_sends():
        sent(WC, wall.at[pl.ds(1, nl - 1), pl.ds(1, nc - 1), core])
        sent(WM, wall.at[pl.ds(1, nl - 1), :, core])
        sent(ZC, zc.at[:, core])
        sent(MM, mub.at[:, chip, core])
        sent(MC, mub.at[:, pl.ds(1, nc - 1)])
        sent(RS, srs.at[:, pl.ds(1, nc - 1)])
        sent(AG, e.at[:, core, pl.ds(1, nc - 1)])
        sent(EX, e.at[:, core])
        sent(LB, lossb.at[pl.ds(1, nb - 1)])

    @pl.when(s < nj)
    def _():
        xbuf[...] = x_ref[:, pl.ds(pl.multiple_of(block * BLOCK, BLOCK), BLOCK)]
        for l in range(nl):
            others(spread_chips)(l)
        last = nl - 1
        for t in range(nl + 7):
            for stage, delay in ((others(spread_mate), 0), (forward, 1), (gram, 2), (reduce, 3), (slopes, 5), (swap, 7), (pull, 8)):
                l = t - delay
                if 0 <= l < nl and not (stage is swap and l == last) and not (stage is pull and l >= last):
                    stage(l)
        swap(last)
        loss_plane()
        pull(last)
        backward()
        early_sends()
        sent(GO, gout.at[:, pl.ds(1, nl - 1)])
        sent(LZ, lossw.at[pl.ds(1, nl - 1)])

    def sent_layer(j):
        sent(WZ, w_ref.at[j, chip, core], j)
        sent(PP, ppo.at[j], j)
    planes(sent_layer)

    def arrived(j):
        got(LZ, j, lossz.at[j])
        for g in range(BLOCK // GROUP):
            got(GO, g * nl + j, outv.at[j, g])
    planes(arrived)
    loss_ref[0, 0] = jnp.sum(jnp.sum(lossz[...], axis=0)) * (1.0 / (nl * nj * BLOCK))
    for j in range(nj):
        for g in range(BLOCK // GROUP):
            out_ref[:, j * BLOCK + g * GROUP:j * BLOCK + (g + 1) * GROUP] = outv[j, g]


def shards(nl, nb, images, weights, bn_mean, bn_var, bn_gain, bn_bias):
    rows, channels = images.shape[1:]
    nj = channels // BLOCK
    nc = nb // 2
    own_rows = rows // nl
    piece = GROUP // nc
    vmem, dma = pltpu.VMEM, pltpu.SemaphoreType.DMA
    halves = BLOCK // GROUP
    out, loss = pl.pallas_call(
        functools.partial(kernel, nl, nb, nj),
        out_shape=(jax.ShapeDtypeStruct((own_rows, channels), BF16),
                   jax.ShapeDtypeStruct((1, 1), F32)),
        in_specs=[pl.BlockSpec(memory_space=vmem)] * 6,
        out_specs=(pl.BlockSpec(memory_space=vmem), pl.BlockSpec(memory_space=pltpu.SMEM)),
        scratch_shapes=[
            vmem((nl, nc, 2, BLOCK // nb, GROUP), BF16),
            vmem((nl, 4, BLOCK), F32),
            vmem((nj, 4, BLOCK), F32),
            vmem((rows, BLOCK), BF16),
            vmem((nl, rows, BLOCK), F32),
            vmem((nl, rows, BLOCK), F32),
            vmem((nl, 2, halves, rows, GROUP), BF16),
            vmem((nl, nc, piece, WIDE), F32),
            vmem((nl, nc, piece, WIDE), BF16),
            vmem((nl, nc, piece, WIDE), BF16),
            vmem((nl, 2, nc, piece, WIDE), BF16),
            vmem((nl, rows, BLOCK), BF16),
            vmem((halves, nl, own_rows, GROUP), BF16),
            vmem((nj, halves, own_rows, GROUP), BF16),
            vmem((nl, nc, 2, 1, BLOCK), F32),
            vmem((1, BLOCK), F32),
            vmem((nb, 8, 128), F32),
            vmem((nj, 8, 128), F32),
            vmem((nl, 8, 128), F32),
            dma((13, nj)),
            dma((13, 2 * nl)),
        ],
        compiler_params=pltpu.CompilerParams(
            collective_id=0, has_side_effects=True, vmem_limit_bytes=60 * 1024 * 1024),
    )(images[0], weights.reshape(nj, nc, 2, BLOCK // nb, GROUP), bn_mean, bn_var, bn_gain, bn_bias)
    return (out[None], loss.reshape(()))


def solution(mesh):
    placed = (
        P("batch", None, None),
        P("section", None, None, None),
        P("section", None),
        P("section", None),
        P("section", None),
        P("section", None),
    )
    return jax.shard_map(
        functools.partial(shards, mesh.shape["section"], mesh.shape["batch"]),
        mesh=mesh,
        in_specs=placed,
        out_specs=(P("batch", "section", None), P()),
        check_vma=False,
    )
```
